128 devices in a mesh: gz: 2 (over x_lo), ma: 64 (over z, y, x_hi, core).
Axes of the slice: x: 4 (x_hi: 2, x_lo: 2; x = x_hi * 2 + x_lo), y: 4, z: 4, core: 2. Of those that a mesh axis runs over, the one named last changes fastest.
Arguments:
- fields: bfloat16 [384, 3, 512, 1024], P('gz', None, 'ma'), may hold values from -6 to 6
- radial_tables: bfloat16 [512, 512, 512], P('ma'), may hold values from -0.25 to 0.25
- radial_counts: int32 [512], replicated, may hold values from 1 to 512, as said below
- assignment: int32 [128], replicated, may hold values from 0 to 127, each once
- depth_analysis: bfloat16 [3, 384, 384], replicated, may hold values from -0.3125 to 0.3125
- synthesis: bfloat16 [3, 384, 384], replicated, may hold values from -0.3125 to 0.3125
- tau_values: float32 [3, 384], replicated, may hold values from 0.1 to 40
- time_steps: float32 [3], replicated, may hold values from 0.05 to 0.5
Outputs:
- coefficients: bfloat16 [384, 3, 1024, 512], P('gz', None, 'ma')
The draws below stay inside these ranges and needn't reach their ends.
Inputs may be any that keep to these rules, and one draw needn't show every extreme that they name: radial_counts[m] is the number of radial modes kept for wavenumber m; wavenumber 0 keeps all 512. `assignment`: every block number appears exactly once.
All inputs are finite; a program needn't handle non-finite values.
Results may differ from the reference program's by a relative error of at most 0.018.
Values may be sent and summed in bfloat16 or wider, within the bound.
No kernel may reach another device: no remote copies, remote signals or barrier semaphores. Data moves between devices by JAX's collectives and lax.ppermute only.
A program may use at most 192 MiB of HBM per device.

```python
import math
import jax
import jax.numpy as jnp
from jax import lax

NPHI = 1024
MMODES = 512
RGRID = 512
NRAD = 512
NZ = 384
NK = 384
FIELDS = 3
MBLOCKS = 128
N_GZ = 2


def draw_radial_counts(key, part):
    key = jax.random.fold_in(key, 7)
    mode_index = jnp.arange(MMODES, dtype=jnp.int32)
    baseline = NRAD - mode_index * NRAD // MMODES
    jitter = jax.random.randint(key, (MMODES,), -3, 4)
    clipped = jnp.clip(baseline + jitter, 1, NRAD)
    return jnp.where(mode_index == 0, NRAD, clipped).astype(jnp.int32)


def level_of(own_key, dims, shards, low, largest):
    gain, own = 1.0, jax.random.fold_in(own_key, 6)
    for axis_at, parts in shards:
        heights = jnp.exp(jax.random.uniform(jax.random.fold_in(own, axis_at), (parts,), jnp.float32, low / len(shards), largest / len(shards)))
        gain = gain * jnp.repeat(heights, dims[axis_at] // parts).reshape([-1 if axis == axis_at else 1 for axis in range(len(dims))])
    return gain


def bell_draw(key, shape, width, limit, split=(), kind=jnp.bfloat16):
    level = level_of(key, shape, split, -0.22, 0.18) if split else 1.0
    values = jax.random.normal(key, shape, jnp.float32) * width * level
    return jnp.minimum(jnp.maximum(values, -limit), limit).astype(kind)


def setup_inputs(seed: int = 0) -> dict:
    key_of = jax.random.split(jax.random.key(seed), 9)
    fields = bell_draw(key_of[0], (NZ, FIELDS, RGRID, NPHI), 1.0, 6.0, ((0, 2), (2, 64)))
    radial_tables = bell_draw(key_of[1], (MMODES, RGRID, NRAD), RGRID ** -0.5, 0.25, ((0, 64),))
    radial_counts = draw_radial_counts(jax.random.fold_in(key_of[8], 71), 0)
    assignment = jax.random.permutation(key_of[3], MBLOCKS).astype(jnp.int32)
    depth_analysis = bell_draw(key_of[4], (FIELDS, NK, NZ), NZ ** -0.5, 0.3125)
    synthesis = bell_draw(key_of[5], (FIELDS, NK, NK), NK ** -0.5, 0.3125)
    tau_values = jnp.clip(jnp.exp(jax.random.uniform(key_of[6], (FIELDS, NK), jnp.float32, math.log(0.1), math.log(40.0))), 0.1, 40.0)
    time_steps = jnp.clip(jnp.exp(jax.random.uniform(key_of[7], (FIELDS,), jnp.float32, math.log(0.05), math.log(0.5))), 0.05, 0.5)
    return dict(fields=fields, radial_tables=radial_tables, radial_counts=radial_counts, assignment=assignment, depth_analysis=depth_analysis, synthesis=synthesis, tau_values=tau_values, time_steps=time_steps)


def slot_modes(assignment, mode_count):
    block_count = assignment.shape[0]
    block_size = mode_count // block_count
    slot_index = jnp.arange(mode_count, dtype=jnp.int32)
    owner_block = slot_index // block_size
    chosen = lax.optimization_barrier(jnp.sum(jnp.where(owner_block[:, None] == jnp.arange(block_count, dtype=jnp.int32)[None, :], assignment[None, :], 0), axis=1))
    return (chosen * block_size + slot_index % block_size).astype(jnp.int32)

def azimuth_table(mode_list, grid_size):
    grid_points = jnp.arange(grid_size, dtype=jnp.int32)
    phase_index = grid_points[:, None] * mode_list[None, :] % grid_size
    angle_values = phase_index.astype(jnp.float32) * (2.0 * math.pi / grid_size)
    norm_scale = math.sqrt(2.0 / grid_size)
    stacked = jnp.stack([jnp.cos(angle_values) * norm_scale, -jnp.sin(angle_values) * norm_scale], axis=2)
    return stacked.reshape(grid_size, 2 * mode_list.shape[0]).astype(jnp.bfloat16)

def kept_counts(mode_list, radial_counts, mode_count):
    matches = mode_list[:, None] == jnp.arange(mode_count, dtype=jnp.int32)[None, :]
    return lax.optimization_barrier(jnp.sum(jnp.where(matches, radial_counts[None, :], 0), axis=1)).astype(jnp.int32)

def mode_weights(column_modes, radial_size):
    summed = column_modes[:, None] + 2 * jnp.arange(radial_size, dtype=jnp.int32)[None, :]
    return (summed * (summed + 2)).astype(jnp.float32) / float(radial_size * radial_size)

def reference(fields, radial_tables, radial_counts, assignment, depth_analysis, synthesis, tau_values, time_steps):
    mode_list = slot_modes(assignment, MMODES)
    phase_table = azimuth_table(mode_list, NPHI)
    counts_here = kept_counts(mode_list, radial_counts, MMODES)
    kept_mask = jnp.arange(NRAD, dtype=jnp.int32)[None, :] < counts_here[:, None]
    radial_eigen = mode_weights(jnp.repeat(mode_list, 2), NRAD)
    depth_local = NZ // N_GZ
    tables = radial_tables.astype(jnp.float32)
    results = []
    for field_index in range(FIELDS):
        flattened = fields[:, field_index].reshape(NZ * RGRID, NPHI)
        azimuthal = jnp.dot(flattened, phase_table, preferred_element_type=jnp.float32).astype(jnp.bfloat16)
        azimuthal = azimuthal.reshape(NZ, RGRID, MMODES, 2).astype(jnp.float32)
        radial = jnp.einsum('zrmp,mrn->mpzn', azimuthal, tables)
        radial = jnp.where(kept_mask[:, None, None, :], radial, 0.0).astype(jnp.bfloat16)
        radial = radial.reshape(2 * MMODES, NZ, NRAD).astype(jnp.float32)
        analysis = depth_analysis[field_index].astype(jnp.float32)
        projected = jnp.zeros((NK, 2 * MMODES, NRAD), jnp.float32)
        for group_index in range(N_GZ):
            depth_start = group_index * depth_local
            partial_value = jnp.einsum('kz,czn->kcn', analysis[:, depth_start:depth_start + depth_local], radial[:, depth_start:depth_start + depth_local])
            projected = projected + lax.optimization_barrier(partial_value.astype(jnp.bfloat16)).astype(jnp.float32)
        divisor = 1.0 + time_steps[field_index] * (radial_eigen[None, :, :] + tau_values[field_index][:, None, None])
        eigen_coef = (projected / divisor).astype(jnp.bfloat16)
        coefficient = jnp.einsum('jk,kcn->jcn', synthesis[field_index].astype(jnp.float32), eigen_coef.astype(jnp.float32))
        results.append(coefficient.astype(jnp.bfloat16))
    return jnp.stack(results, axis=1)
```

```python
import functools
import math

import jax
import jax.numpy as jnp
from jax import lax
from jax.experimental import pallas as pl
from jax.experimental.pallas import tpu as pltpu
from jax.sharding import Mesh
from jax.sharding import PartitionSpec as P

F32, BF16 = jnp.float32, jnp.bfloat16
NT = (((1,), (1,)), ((), ()))
NN = (((1,), (0,)), ((), ()))
MIB = 1 << 20
ORDER = ("z", "y", "core", "xh", "xl")


def dot(a, b, dims):
    return lax.dot_general(a, b, dims, preferred_element_type=F32)


def params(mib):
    return pltpu.CompilerParams(vmem_limit_bytes=mib * MIB)


def phase_kernel(c0_ref, s0_ref, c1_ref, s1_ref, out_ref):
    c0, s0 = c0_ref[...], s0_ref[...]
    width = c0.shape[1]
    for block in range(out_ref.shape[2] // width):
        c1, s1 = c1_ref[:, block : block + 1], s1_ref[:, block : block + 1]
        lanes = slice(block * width, (block + 1) * width)
        out_ref[0, :, lanes] = (c0 * c1 - s0 * s1).astype(BF16)
        out_ref[1, :, lanes] = -(s0 * c1 + c0 * s1).astype(BF16)


def phase_rows(modes, grid_size):
    width = 128

    def tables(points, scale):
        index = (modes[:, None] * points[None, :]) % grid_size
        angle = index.astype(F32) * (2.0 * math.pi / grid_size)
        return jnp.cos(angle) * scale, jnp.sin(angle) * scale

    c0, s0 = tables(jnp.arange(width, dtype=jnp.int32), math.sqrt(2.0 / grid_size))
    c1, s1 = tables(jnp.arange(grid_size // width, dtype=jnp.int32) * width, 1.0)
    return pl.pallas_call(
        phase_kernel,
        out_shape=jax.ShapeDtypeStruct((2, modes.shape[0], grid_size), BF16),
        compiler_params=params(32),
        name="phase_table",
    )(c0, s0, c1, s1)


def azimuth_kernel(phase_ref, x_ref, out_ref, wide, rows, spread):
    depth, radii, _ = x_ref.shape
    pad = 256 - depth
    wide[...] = x_ref[...].astype(F32)
    zeros = jnp.zeros((pad, x_ref.shape[2]), BF16)
    for r in range(radii):
        rows[r, 0:pad] = zeros
        rows[r, pad : pad + depth] = wide[:, r, :].astype(BF16)
        rows[r, pad + depth :] = zeros
    for r in range(radii):
        cosine = dot(phase_ref[0], rows[r, pad:], NT)
        sine = dot(phase_ref[1], rows[r, 0:256], NT)
        spread[:, r, 0:128] = cosine[:, :128]
        spread[:, r, 128:256] = cosine[:, 128:] + sine[:, :128]
        spread[:, r, 256:384] = sine[:, 128:]
    out_ref[...] = spread[...].astype(BF16)


def azimuth(phase, fields, field):
    depth, _, radii, grid_size = fields.shape
    slots = phase.shape[1]
    whole = lambda shape: pl.BlockSpec(shape, lambda i: (0,) * len(shape))
    return pl.pallas_call(
        azimuth_kernel,
        grid=(1,),
        in_specs=[
            whole(phase.shape),
            pl.BlockSpec((depth, None, radii, grid_size), lambda i: (0, field, 0, 0)),
        ],
        out_specs=whole((slots, radii, 2 * depth)),
        out_shape=jax.ShapeDtypeStruct((slots, radii, 2 * depth), BF16),
        scratch_shapes=[
            pltpu.VMEM((depth, radii, grid_size), F32),
            pltpu.VMEM((radii, 512 - depth, grid_size), BF16),
            pltpu.VMEM((slots, radii, 2 * depth), F32),
        ],
        compiler_params=params(56),
        cost_estimate=pl.CostEstimate(
            flops=2 * 2 * slots * radii * 256 * grid_size, bytes_accessed=9 * MIB, transcendentals=0
        ),
        name="azimuth",
    )(phase, fields)


def solve_kernel(
    place_ref, modes_ref, x_ref, table_ref, depth_ref, synth_ref, tau_ref, step_ref, *rest
):
    own_ref, other_ref, spread = rest[-3:]
    pairs, groups, slots, radii, lanes = x_ref.shape
    modes_here = table_ref.shape[1]
    half = own_ref.shape[0]
    step = step_ref[0, 0]
    n_index = lax.broadcasted_iota(jnp.int32, (modes_here, 1), 0) + pl.program_id(0) * modes_here
    tau = 1.0 + step * tau_ref[...]
    for q in range(slots):
        projected = [None, None]
        for g in range(groups):
            x = x_ref[:, g, q].reshape(pairs * radii, lanes)
            radial = dot(table_ref[q], x, NN).astype(BF16)
            for p in range(2):
                term = dot(radial[:, p * 128 : p * 128 + 256], depth_ref[p, g], NN)
                projected[p] = term if g == 0 else projected[p] + term
        summed = modes_ref[q] + 2 * n_index
        weight = (summed * (summed + 2)).astype(F32) * (step / float(512 * 512))
        scale = 1.0 / (weight + tau)
        for p in range(2):
            eigen = (projected[p] * scale).astype(BF16)
            spread[:, 2 * q + p, :] = dot(synth_ref[...], eigen, NT)
    own_ref[...] = spread[:half].astype(BF16)
    other_ref[...] = spread[half:].astype(BF16)


def solve(place, modes, x, table, depth, synth, tau, steps, field, out):
    depth_total = synth.shape[1]
    slots, radial_size, _ = table.shape
    half, cols = depth_total // 2, 2 * slots
    fields = synth.shape[0]
    block = 256
    const = lambda shape: pl.BlockSpec(shape, lambda i, *_: (0,) * len(shape))
    of_field = lambda *shape: pl.BlockSpec((None, *shape), lambda i, *_: (field,) + (0,) * len(shape))
    in_specs = [
        const(x.shape),
        pl.BlockSpec((slots, block, table.shape[2]), lambda i, *_: (0, i, 0)),
        of_field(*depth.shape[1:]),
        of_field(depth_total, depth_total),
        of_field(1, depth_total),
        of_field(1, 1),
    ]
    args = [place, modes, x, table, depth, synth, tau[:, None, :], steps[:, None, None]]
    aliases = {}
    if out is not None:
        in_specs.append(pl.BlockSpec(memory_space=pl.ANY))
        args.append(out)
        aliases = {len(args) - 1: 0}
    return pl.pallas_call(
        solve_kernel,
        grid_spec=pltpu.PrefetchScalarGridSpec(
            num_scalar_prefetch=2,
            grid=(radial_size // block,),
            in_specs=in_specs,
            out_specs=[
                pl.BlockSpec((half, None, cols, block), lambda i, place, _: (0, field, place[0], i)),
                pl.BlockSpec((half, cols, block), lambda i, *_: (0, 0, i)),
            ],
            scratch_shapes=[pltpu.VMEM((depth_total, cols, block), F32)],
        ),
        out_shape=[
            jax.ShapeDtypeStruct((half, fields, 2 * cols, radial_size), BF16),
            jax.ShapeDtypeStruct((half, cols, radial_size), BF16),
        ],
        input_output_aliases=aliases,
        compiler_params=params(56),
        cost_estimate=pl.CostEstimate(flops=6 * 10**9, bytes_accessed=10 * MIB, transcendentals=0),
        name="solve",
    )(*args)


def place_kernel(place_ref, received_ref, _, out_ref):
    out_ref[...] = received_ref[...]


def put(place, received, field, out):
    half, cols, radial_size = received.shape
    return pl.pallas_call(
        place_kernel,
        grid_spec=pltpu.PrefetchScalarGridSpec(
            num_scalar_prefetch=1,
            grid=(4,),
            in_specs=[
                pl.BlockSpec((half // 4, cols, radial_size), lambda i, _: (i, 0, 0)),
                pl.BlockSpec(memory_space=pl.ANY),
            ],
            out_specs=pl.BlockSpec(
                (half // 4, None, cols, radial_size), lambda i, place: (i, field, 1 - place[0], 0)
            ),
        ),
        out_shape=jax.ShapeDtypeStruct(out.shape, BF16),
        input_output_aliases={2: 0},
        compiler_params=params(32),
        cost_estimate=pl.CostEstimate(flops=0, bytes_accessed=4 * MIB, transcendentals=0),
        name="put",
    )(place, received, out)


def shards(
    fields,
    radial_tables,
    radial_counts,
    assignment,
    depth_analysis,
    synthesis,
    tau_values,
    time_steps,
):
    depth_local, field_count, radii, grid_size = fields.shape
    depth_total = depth_analysis.shape[1]
    mode_count = grid_size // 2
    block_count = assignment.shape[0]
    block_size = mode_count // block_count
    group = lax.axis_index("xl")
    ring = lax.axis_index(("z", "y", "xh", "core"))
    place = group[None].astype(jnp.int32)
    inner = jnp.arange(block_size, dtype=jnp.int32)

    ordered = assignment.reshape(16, 2, 2, 2).transpose(0, 2, 1, 3).reshape(block_count)
    modes_to = (ordered[:, None] * block_size + inner[None, :]).reshape(mode_count)
    phase = phase_rows(modes_to, grid_size)

    own_block = lax.dynamic_slice_in_dim(assignment, ring * 2 + group, 1)
    modes_here = own_block * block_size + inner
    hit = modes_here[:, None] == jnp.arange(mode_count, dtype=jnp.int32)[None, :]
    counts_here = jnp.sum(jnp.where(hit, radial_counts[None, :], 0), axis=1)
    table = lax.dynamic_slice_in_dim(radial_tables, group * block_size, block_size, 0)
    radial_total, radial_size = table.shape[1:]
    table = table.reshape(block_size, 16, 2, 2, radii, radial_size)
    table = table.transpose(0, 5, 1, 3, 2, 4).reshape(block_size, radial_size, radial_total)
    kept = jnp.arange(radial_size, dtype=jnp.int32)[None, :] < counts_here[:, None]
    table = jnp.where(kept[:, :, None], table, jnp.zeros((), BF16))

    pad = 256 - depth_local
    by_group = depth_analysis.reshape(field_count, depth_total, 2, depth_local).transpose(0, 2, 3, 1)
    low = jnp.pad(by_group, ((0, 0), (0, 0), (0, pad), (0, 0)))
    high = jnp.pad(by_group, ((0, 0), (0, 0), (pad, 0), (0, 0)))
    depth = jnp.stack([low, high], axis=1)
    half = depth_total // 2
    mine = lax.dynamic_slice_in_dim(synthesis, group * half, half, 1)
    theirs = lax.dynamic_slice_in_dim(synthesis, (1 - group) * half, half, 1)
    synth = jnp.concatenate([mine, theirs], axis=1)

    received = []
    for field in range(field_count):
        sent = azimuth(phase, fields, field)
        sent = sent.reshape(block_count, block_size, radii, 2 * depth_local)
        received.append(lax.all_to_all(sent, ORDER, 0, 0, tiled=True))
    out, others = None, []
    for field in range(field_count):
        x = received[field].reshape(block_count // 2, 2, block_size, radii, 2 * depth_local)
        out, other = solve(
            place, modes_here, x, table, depth, synth, tau_values, time_steps, field, out
        )
        others.append(lax.ppermute(other, "xl", [(0, 1), (1, 0)]))
    for field in range(field_count):
        out = put(place, others[field], field, out)
    return out


def solution(mesh):
    split = Mesh(mesh.devices.reshape(2, 4, 4, 2, 2), ("xl", "z", "y", "xh", "core"))
    ma = ("z", "y", "xh", "core")
    placed = (P("xl", None, ma, None), P(ma, None, None), P(), P(), P(), P(), P(), P())
    return jax.shard_map(
        shards, mesh=split, in_specs=placed, out_specs=P("xl", None, ma, None), check_vma=False
    )
```

```python
import functools
import math

import jax
import jax.numpy as jnp
from jax import lax
from jax.experimental import pallas as pl
from jax.experimental.pallas import tpu as pltpu
from jax.sharding import Mesh
from jax.sharding import PartitionSpec as P

F32, BF16 = jnp.float32, jnp.bfloat16
NT = (((1,), (1,)), ((), ()))
NN = (((1,), (0,)), ((), ()))
MIB = 1 << 20


def cost(micros):
    return pl.CostEstimate(flops=micros * 10**9, bytes_accessed=1000, transcendentals=0)


COSTS = {'azB': 0, 'azC': 20, 'joinA': 0, 'joinB': 20, 'joinC': 0, 's0a': 0, 's0b': 80, 's1a': 0, 's1b': 0, 's2a': 0, 's2b': 0, 'p0a': 20, 'p0b': 20, 'p1a': 1, 'p1b': 1, 'p2a': 1, 'p2b': 1}
SHORT = cost(0)
SHIFTS = (1, 3, 2, 0)


def along(x, shift):
    at = lambda chip: (chip % 2) * 2 + chip // 2
    return lax.ppermute(x, ("xl", "xh"), [(at(i), at((i + shift) % 4)) for i in range(4)])


def dot(a, b, dims):
    return lax.dot_general(a, b, dims, preferred_element_type=F32)


def params(mib):
    return pltpu.CompilerParams(vmem_limit_bytes=mib * MIB)


def phase_kernel(c0_ref, s0_ref, c1_ref, s1_ref, out_ref):
    c0, s0 = c0_ref[...], s0_ref[...]
    width = c0.shape[1]
    for block in range(out_ref.shape[2] // width):
        c1, s1 = c1_ref[:, block : block + 1], s1_ref[:, block : block + 1]
        lanes = slice(block * width, (block + 1) * width)
        out_ref[0, :, lanes] = (c0 * c1 - s0 * s1).astype(BF16)
        out_ref[1, :, lanes] = -(s0 * c1 + c0 * s1).astype(BF16)


def phase_rows(modes, grid_size):
    width = 128

    def tables(points, scale):
        index = (modes[:, None] * points[None, :]) % grid_size
        angle = index.astype(F32) * (2.0 * math.pi / grid_size)
        return jnp.cos(angle) * scale, jnp.sin(angle) * scale

    c0, s0 = tables(jnp.arange(width, dtype=jnp.int32), math.sqrt(2.0 / grid_size))
    c1, s1 = tables(jnp.arange(grid_size // width, dtype=jnp.int32) * width, 1.0)
    return pl.pallas_call(
        phase_kernel,
        out_shape=jax.ShapeDtypeStruct((2, modes.shape[0], grid_size), BF16),
        compiler_params=params(40),
        cost_estimate=SHORT,
        name="phase_table",
    )(c0, s0, c1, s1)


def azimuth_kernel(many, phase_ref, swap_ref, x_ref, *rest):
    outs, (rows, spread) = rest[many:-2], rest[-2:]
    depth, radii, grid_size = x_ref.shape
    pad = 256 - depth
    group = 256 // radii

    @pl.when(pl.program_id(0) == 0)
    def _():
        zeros = jnp.zeros((pad, grid_size), BF16)
        for r in range(radii):
            rows[r, 0:pad] = zeros
            rows[r, pad + depth :] = zeros
        for block in range(depth // group):
            heights = slice(block * group, (block + 1) * group)
            swapped = dot(swap_ref[...], x_ref[heights].reshape(256, grid_size), NN).astype(BF16)
            for r in range(radii):
                start = pad + block * group
                rows[r, start : start + group] = swapped[r * group : (r + 1) * group]

    for r in range(radii):
        cosine = dot(phase_ref[0], rows[r, pad:], NT)
        sine = dot(phase_ref[1], rows[r, 0:256], NT)
        spread[:, r, 0:128] = cosine[:, :128]
        spread[:, r, 128:256] = cosine[:, 128:] + sine[:, :128]
        spread[:, r, 256:384] = sine[:, 128:]
    count = spread.shape[0] // len(outs)
    for j, out in enumerate(outs):
        piece = spread[j * count : (j + 1) * count].astype(BF16)
        out[...] = piece.reshape(out.shape)


def azimuth(phase, swap, fields, field, halves, *after, micros=0):
    depth, _, radii, grid_size = fields.shape
    first, count = halves
    rows = phase.shape[1] // 2
    piece = (rows // 8, 2, radii, 2 * depth)
    whole = lambda shape: pl.BlockSpec(shape, lambda i: (0,) * len(shape))
    return pl.pallas_call(
        functools.partial(azimuth_kernel, len(after)),
        grid=(count,),
        in_specs=[
            pl.BlockSpec((2, rows, grid_size), lambda i: (0, first + i, 0)),
            whole(swap.shape),
            pl.BlockSpec((depth, None, radii, grid_size), lambda i: (0, field, 0, 0)),
            *([pl.BlockSpec(memory_space=pl.ANY)] * len(after)),
        ],
        out_specs=[pl.BlockSpec(piece, lambda i: (0, i, 0, 0))] * 4,
        out_shape=[jax.ShapeDtypeStruct((piece[0], 2 * count, *piece[2:]), BF16)] * 4,
        scratch_shapes=[
            pltpu.VMEM((radii, 512 - depth, grid_size), BF16),
            pltpu.VMEM((rows, radii, 2 * depth), F32),
        ],
        compiler_params=params(48),
        cost_estimate=cost(micros),
        name="azimuth",
    )(phase, swap, fields, *after)


def join_kernel(*refs):
    for at, piece in enumerate(refs[:4]):
        refs[-1][:, at] = piece[...]


def join(pieces, *after, micros=0):
    steps = 2
    shape = pieces[0].shape
    block = (shape[0] // steps, *shape[1:])
    return pl.pallas_call(
        join_kernel,
        grid=(steps,),
        in_specs=[pl.BlockSpec(block, lambda i: (i, 0, 0, 0))] * 4
        + [pl.BlockSpec(memory_space=pl.ANY)] * len(after),
        out_specs=pl.BlockSpec((block[0], 4, *block[1:]), lambda i: (i, 0, 0, 0, 0)),
        out_shape=jax.ShapeDtypeStruct((shape[0], 4, *shape[1:]), BF16),
        compiler_params=params(62),
        cost_estimate=cost(micros),
        name="join",
    )(*pieces, *after)


def tie(x, *after):
    anywhere = pl.BlockSpec(memory_space=pl.ANY)
    return pl.pallas_call(
        lambda *_: None,
        in_specs=[anywhere] * (1 + len(after)),
        out_specs=anywhere,
        out_shape=jax.ShapeDtypeStruct(x.shape, x.dtype),
        input_output_aliases={0: 0},
        cost_estimate=SHORT,
        name="tie",
    )(x, *after)


def solve_kernel(
    first, many, place_ref, modes_ref, *rest
):
    xs, (table_ref, depth_ref, synth_ref, tau_ref, step_ref) = rest[:many], rest[many : many + 5]
    own_ref, other_ref, spread = rest[-3:]
    sources, _, some, radii, lanes = xs[0].shape
    slots = table_ref.shape[0]
    modes_here = table_ref.shape[2]
    near = 1 - place_ref[0]
    half = own_ref.shape[0]
    step = step_ref[0, 0]
    block = first + pl.program_id(0)
    n_index = lax.broadcasted_iota(jnp.int32, (modes_here, 1), 0) + block * modes_here
    tau = 1.0 + step * tau_ref[...]
    for q in range(slots):
        projected = [None, None]
        x = xs[q // some]
        for g, parts in enumerate((((0, 3), (1, 2)), ((near, 0), (1 - near, 1)))):
            radial = sum(
                dot(table_ref[q, side], x[:, at, q % some].reshape(sources * radii, lanes), NN)
                for side, at in parts
            ).astype(BF16)
            for p in range(2):
                term = dot(radial[:, p * 128 : p * 128 + 256], depth_ref[p, g], NN)
                projected[p] = term if g == 0 else projected[p] + term
        summed = modes_ref[q] + 2 * n_index
        weight = (summed * (summed + 2)).astype(F32) * (step / float(512 * 512))
        scale = 1.0 / (weight + tau)
        for p in range(2):
            eigen = (projected[p] * scale).astype(BF16)
            spread[:, 2 * q + p, :] = dot(synth_ref[...], eigen, NT)
    own_ref[...] = spread[:half].astype(BF16)
    other_ref[...] = spread[half:].astype(BF16)


def solve(place, modes, xs, table, depth, synth, tau, steps, field, out, blocks, *after, micros=0):
    depth_total = synth.shape[1]
    slots, _, radial_size, _ = table.shape
    half, cols = depth_total // 2, 2 * slots
    fields = synth.shape[0]
    block = 256
    first, count = blocks
    const = lambda shape: pl.BlockSpec(shape, lambda i, *_: (0,) * len(shape))
    of_field = lambda *shape: pl.BlockSpec((None, *shape), lambda i, *_: (field,) + (0,) * len(shape))

    in_specs = [
        *(const(x.shape) for x in xs),
        pl.BlockSpec((slots, 2, block, table.shape[3]), lambda i, *_: (0, 0, first + i, 0)),
        of_field(*depth.shape[1:]),
        of_field(depth_total, depth_total),
        of_field(1, depth_total),
        of_field(1, 1),
    ]
    args = [place, modes, *xs, table, depth, synth, tau[:, None, :], steps[:, None, None]]
    aliases = {}
    if out is not None:
        in_specs.append(pl.BlockSpec(memory_space=pl.ANY))
        args.append(out)
        aliases = {len(args) - 1: 0}
    in_specs += [pl.BlockSpec(memory_space=pl.ANY)] * len(after)
    args += after
    return pl.pallas_call(
        functools.partial(solve_kernel, first, len(xs)),
        grid_spec=pltpu.PrefetchScalarGridSpec(
            num_scalar_prefetch=2,
            grid=(count,),
            in_specs=in_specs,
            out_specs=[
                pl.BlockSpec((half, None, cols, block), lambda i, place, _: (0, field, place[0], first + i)),
                pl.BlockSpec((half, cols, block), lambda i, *_: (0, 0, i)),
            ],
            scratch_shapes=[pltpu.VMEM((depth_total, cols, block), F32)],
        ),
        out_shape=[
            jax.ShapeDtypeStruct((half, fields, 2 * cols, radial_size), BF16),
            jax.ShapeDtypeStruct((half, cols, count * block), BF16),
        ],
        input_output_aliases=aliases,
        compiler_params=params(62),
        cost_estimate=cost(micros),
        name="solve",
    )(*args)


def place_kernel(place_ref, received_ref, _, out_ref):
    out_ref[...] = received_ref[...]


def put(place, received, field, first, out, micros):
    half, cols, radial_size = received.shape
    return pl.pallas_call(
        place_kernel,
        grid_spec=pltpu.PrefetchScalarGridSpec(
            num_scalar_prefetch=1,
            grid=(1,),
            in_specs=[
                pl.BlockSpec((half, cols, radial_size), lambda i, _: (i, 0, 0)),
                pl.BlockSpec(memory_space=pl.ANY),
            ],
            out_specs=pl.BlockSpec(
                (half, None, cols, radial_size), lambda i, place: (i, field, 1 - place[0], first)
            ),
        ),
        out_shape=jax.ShapeDtypeStruct(out.shape, BF16),
        input_output_aliases={2: 0},
        compiler_params=params(62),
        cost_estimate=cost(micros),
        name="put",
    )(place, received, out)


def shards(
    fields,
    radial_tables,
    radial_counts,
    assignment,
    depth_analysis,
    synthesis,
    tau_values,
    time_steps,
):
    depth_local, field_count, radii, grid_size = fields.shape
    depth_total = depth_analysis.shape[1]
    mode_count = grid_size // 2
    block_count = assignment.shape[0]
    block_size = mode_count // block_count
    group, upper = lax.axis_index("xl"), lax.axis_index("xh")
    ring = lax.axis_index(("z", "y", "xh", "core"))
    place = group[None].astype(jnp.int32)
    inner = jnp.arange(block_size, dtype=jnp.int32)

    by_x = assignment.reshape(16, 2, 2, 2).transpose(1, 3, 0, 2).reshape(4, 32)
    by_x = lax.dynamic_slice_in_dim(jnp.concatenate([by_x, by_x]), 2 * upper + group, 4)
    ordered = jnp.stack([by_x[shift] for shift in SHIFTS])
    modes_to = ordered[None, :, :, None] * block_size + inner.reshape(2, 1, 1, 2)
    modes_to = modes_to.reshape(mode_count)
    phase = phase_rows(modes_to, grid_size)
    index = jnp.arange(256, dtype=jnp.int32)
    heights = 256 // radii
    origin = (index % heights) * radii + index // heights
    swap = (origin[:, None] == index[None, :]).astype(BF16)

    def along_x(pieces):
        return [along(x, shift) for x, shift in zip(pieces, SHIFTS[:3], strict=True)]

    def across(x):
        return lax.all_to_all(x, ("z", "y", "core"), 0, 0, tiled=True)

    def solved(xs, field, out, blocks, *after, **options):
        operands = (table, depth, synth, tau_values, time_steps, field, out, blocks)
        out, other = solve(place, modes_here, xs, *operands, *after, **options)
        return out, lax.ppermute(other, "xl", [(0, 1), (1, 0)])

    def sent_of(field, halves, *after, **options):
        *moving, own = azimuth(phase, swap, fields, field, halves, *after, **options)
        return [*along_x(moving), own]

    whole, low_n, high_n = (0, 2), (0, 1), (1, 1)
    a = sent_of(0, whole)
    b = sent_of(1, whole, a[3], micros=COSTS["azB"])
    c = sent_of(2, whole, b[3], micros=COSTS["azC"])
    a = join(a, c[3], micros=COSTS["joinA"])

    group, upper = tie(jnp.stack([group, upper]).astype(jnp.int32), a)
    own_block = lax.dynamic_slice_in_dim(assignment, ring * 2 + group, 1)
    modes_here = own_block * block_size + inner
    hit = modes_here[:, None] == jnp.arange(mode_count, dtype=jnp.int32)[None, :]
    counts_here = jnp.sum(jnp.where(hit, radial_counts[None, :], 0), axis=1)
    table = lax.dynamic_slice_in_dim(radial_tables, group * block_size, block_size, 0)
    radial_total, radial_size = table.shape[1:]
    table = table.reshape(block_size, 16, 2, 2, radii, radial_size)
    table = table.transpose(0, 2, 5, 1, 3, 4).reshape(block_size, 2, radial_size, radial_total // 2)
    table = jnp.where(upper == 0, table, table[:, ::-1])
    kept = jnp.arange(radial_size, dtype=jnp.int32)[None, :] < counts_here[:, None]
    table = jnp.where(kept[:, None, :, None], table, jnp.zeros((), BF16))

    pad = 256 - depth_local

    def heights_of(which):
        part = lax.dynamic_slice_in_dim(depth_analysis, which * depth_local, depth_local, 2)
        return part.transpose(0, 2, 1)

    by_group = jnp.stack([heights_of(group), heights_of(1 - group)], axis=1)
    low = jnp.pad(by_group, ((0, 0), (0, 0), (0, pad), (0, 0)))
    high = jnp.pad(by_group, ((0, 0), (0, 0), (pad, 0), (0, 0)))
    depth = jnp.stack([low, high], axis=1)
    half = depth_total // 2
    mine = lax.dynamic_slice_in_dim(synthesis, group * half, half, 1)
    theirs = lax.dynamic_slice_in_dim(synthesis, (1 - group) * half, half, 1)
    synth = jnp.concatenate([mine, theirs], axis=1)

    a = across(a)
    b = join(b, table, depth, synth, micros=COSTS["joinB"])
    out, other0a = solved([a], 0, None, low_n, b, micros=COSTS["s0a"])
    b = across(b)
    out, other0b = solved([a], 0, out, high_n, micros=COSTS["s0b"])
    c = join(c, out, micros=COSTS["joinC"])
    out = put(place, other0a, 0, 0, out, micros=COSTS["p0a"])
    c = across(c)
    out, other1a = solved([b], 1, out, low_n, micros=COSTS["s1a"])
    out = put(place, other0b, 0, 1, out, micros=COSTS["p0b"])
    out, other1b = solved([b], 1, out, high_n, micros=COSTS["s1b"])
    out, other2a = solved([c], 2, out, low_n, micros=COSTS["s2a"])
    out = put(place, other1a, 1, 0, out, micros=COSTS["p1a"])
    out, other2b = solved([c], 2, out, high_n, micros=COSTS["s2b"])
    out = put(place, other1b, 1, 1, out, micros=COSTS["p1b"])
    out = put(place, other2a, 2, 0, out, micros=COSTS["p2a"])
    return put(place, other2b, 2, 1, out, micros=COSTS["p2b"])


def solution(mesh):
    split = Mesh(mesh.devices.reshape(2, 4, 4, 2, 2), ("xl", "z", "y", "xh", "core"))
    ma = ("z", "y", "xh", "core")
    placed = (P("xl", None, ma, None), P(ma, None, None), P(), P(), P(), P(), P(), P())
    return jax.shard_map(
        shards, mesh=split, in_specs=placed, out_specs=P("xl", None, ma, None), check_vma=False
    )
```

```python
import functools
import math

import jax
import jax.numpy as jnp
from jax import lax
from jax.experimental import pallas as pl
from jax.experimental.pallas import tpu as pltpu
from jax.sharding import Mesh
from jax.sharding import PartitionSpec as P

F32, BF16 = jnp.float32, jnp.bfloat16
NT = (((1,), (1,)), ((), ()))
NN = (((1,), (0,)), ((), ()))
MIB = 1 << 20


def cost(micros):
    return pl.CostEstimate(flops=micros * 10**9, bytes_accessed=1000, transcendentals=0)


COSTS = {'vertical': 80, 'tables': 0, 'azB': 0, 'azC': 20, 'azD': 0, 'joinA': 0, 'joinB': 20, 'joinC': 0, 'joinD': 5, 'sA': 0, 's1a': 0, 's1b': 40, 's2a': 0, 's2b': 0, 'sDa': 0, 'sDb': 0, 'p1a': 20, 'p1b': 20, 'p2a': 1, 'p2b': 1, 'mDa': 1, 'mDb': 1}
SHORT = cost(0)
SHIFTS = (1, 3, 2, 0)


def along(x, shift):
    at = lambda chip: (chip % 2) * 2 + chip // 2
    return lax.ppermute(x, ("xl", "xh"), [(at(i), at((i + shift) % 4)) for i in range(4)])


def dot(a, b, dims):
    return lax.dot_general(a, b, dims, preferred_element_type=F32)


def params(mib):
    return pltpu.CompilerParams(vmem_limit_bytes=mib * MIB)


def phase_kernel(c0_ref, s0_ref, c1_ref, s1_ref, out_ref):
    c0, s0 = c0_ref[...], s0_ref[...]
    width = c0.shape[1]
    for block in range(out_ref.shape[2] // width):
        c1, s1 = c1_ref[:, block : block + 1], s1_ref[:, block : block + 1]
        lanes = slice(block * width, (block + 1) * width)
        out_ref[0, :, lanes] = (c0 * c1 - s0 * s1).astype(BF16)
        out_ref[1, :, lanes] = -(s0 * c1 + c0 * s1).astype(BF16)


def phase_rows(modes, grid_size):
    width = 128

    def tables(points, scale):
        index = (modes[:, None] * points[None, :]) % grid_size
        angle = index.astype(F32) * (2.0 * math.pi / grid_size)
        return jnp.cos(angle) * scale, jnp.sin(angle) * scale

    c0, s0 = tables(jnp.arange(width, dtype=jnp.int32), math.sqrt(2.0 / grid_size))
    c1, s1 = tables(jnp.arange(grid_size // width, dtype=jnp.int32) * width, 1.0)
    return pl.pallas_call(
        phase_kernel,
        out_shape=jax.ShapeDtypeStruct((2, modes.shape[0], grid_size), BF16),
        compiler_params=params(40),
        cost_estimate=SHORT,
        name="phase_table",
    )(c0, s0, c1, s1)


def azimuth_kernel(many, phase_ref, swap_ref, x_ref, *rest):
    outs, (rows, spread) = rest[many:-2], rest[-2:]
    depth, radii, grid_size = x_ref.shape
    pad = 256 - depth
    group = 256 // radii

    @pl.when(pl.program_id(0) == 0)
    def _():
        zeros = jnp.zeros((pad, grid_size), BF16)
        for r in range(radii):
            rows[r, 0:pad] = zeros
            rows[r, pad + depth :] = zeros
        for block in range(depth // group):
            heights = slice(block * group, (block + 1) * group)
            swapped = dot(swap_ref[...], x_ref[heights].reshape(256, grid_size), NN).astype(BF16)
            for r in range(radii):
                start = pad + block * group
                rows[r, start : start + group] = swapped[r * group : (r + 1) * group]

    for r in range(radii):
        cosine = dot(phase_ref[0], rows[r, pad:], NT)
        sine = dot(phase_ref[1], rows[r, 0:256], NT)
        spread[:, r, 0:128] = cosine[:, :128]
        spread[:, r, 128:256] = cosine[:, 128:] + sine[:, :128]
        spread[:, r, 256:384] = sine[:, 128:]
    count = spread.shape[0] // len(outs)
    for j, out in enumerate(outs):
        piece = spread[j * count : (j + 1) * count].astype(BF16)
        out[...] = piece.reshape(out.shape)


def azimuth(phase, swap, fields, field, halves, *after, micros=0):
    depth, _, radii, grid_size = fields.shape
    first, count = halves
    rows = phase.shape[1] // 2
    piece = (rows // 8, 2, radii, 2 * depth)
    whole = lambda shape: pl.BlockSpec(shape, lambda i: (0,) * len(shape))
    return pl.pallas_call(
        functools.partial(azimuth_kernel, len(after)),
        grid=(count,),
        in_specs=[
            pl.BlockSpec((2, rows, grid_size), lambda i: (0, first + i, 0)),
            whole(swap.shape),
            pl.BlockSpec((depth, None, radii, grid_size), lambda i: (0, field, 0, 0)),
            *([pl.BlockSpec(memory_space=pl.ANY)] * len(after)),
        ],
        out_specs=[pl.BlockSpec(piece, lambda i: (0, i, 0, 0))] * 4,
        out_shape=[jax.ShapeDtypeStruct((piece[0], 2 * count, *piece[2:]), BF16)] * 4,
        scratch_shapes=[
            pltpu.VMEM((radii, 512 - depth, grid_size), BF16),
            pltpu.VMEM((rows, radii, 2 * depth), F32),
        ],
        compiler_params=params(48),
        cost_estimate=cost(micros),
        name="azimuth",
    )(phase, swap, fields, *after)


def join_kernel(*refs):
    for at, piece in enumerate(refs[:4]):
        refs[-1][:, at] = piece[...]


def join(pieces, *after, micros=0):
    steps = 2
    shape = pieces[0].shape
    block = (shape[0] // steps, *shape[1:])
    return pl.pallas_call(
        join_kernel,
        grid=(steps,),
        in_specs=[pl.BlockSpec(block, lambda i: (i, 0, 0, 0))] * 4
        + [pl.BlockSpec(memory_space=pl.ANY)] * len(after),
        out_specs=pl.BlockSpec((block[0], 4, *block[1:]), lambda i: (i, 0, 0, 0, 0)),
        out_shape=jax.ShapeDtypeStruct((shape[0], 4, *shape[1:]), BF16),
        compiler_params=params(62),
        cost_estimate=cost(micros),
        name="join",
    )(*pieces, *after)


def tables_kernel(own_ref, modes_ref, counts_ref, table_ref, *rest):
    out_ref = rest[-1]
    rows, size = out_ref.shape[1:]
    kept = counts_ref[modes_ref[pl.program_id(0)]]
    n_index = lax.broadcasted_iota(jnp.int32, (rows, 1), 0)
    for side in range(2):
        upper = own_ref[1] if side == 0 else 1 - own_ref[1]
        part = table_ref[:, upper].astype(F32).reshape(size, rows)
        out_ref[side] = jnp.where(n_index < kept, part.T, 0.0).astype(BF16)


def tables(own, modes, counts, radial_tables, radii, *after, micros=0):
    slots, radial_total, radial_size = radial_tables.shape
    slots //= 2
    split = (16, 2, 2, radii, radial_size)
    return pl.pallas_call(
        tables_kernel,
        grid_spec=pltpu.PrefetchScalarGridSpec(
            num_scalar_prefetch=3,
            grid=(slots,),
            in_specs=[
                pl.BlockSpec((None, *split), lambda i, own, *_: (own[0] * slots + i, 0, 0, 0, 0, 0)),
                *([pl.BlockSpec(memory_space=pl.ANY)] * len(after)),
            ],
            out_specs=pl.BlockSpec(
                (None, 2, radial_size, radial_total // 2), lambda i, *_: (i, 0, 0, 0)
            ),
        ),
        out_shape=jax.ShapeDtypeStruct((slots, 2, radial_size, radial_total // 2), BF16),
        compiler_params=params(62),
        cost_estimate=cost(micros),
        name="tables",
    )(own, modes, counts, radial_tables.reshape(2 * slots, *split), *after)


def vertical_kernel(own_ref, depth_ref, synth_ref, *rest):
    by_height, turned, depth_out, synth_out = rest[-1], rest[-2], rest[-4], rest[-3]
    local = synth_ref.shape[0] // 2
    pad = 256 - local
    by_height[...] = depth_ref[...].astype(F32).T.astype(BF16)
    turned[...] = synth_ref[...]
    zeros = jnp.zeros((pad, synth_ref.shape[0]), BF16)
    for side in range(2):
        group = own_ref[0] if side == 0 else 1 - own_ref[0]
        start = pl.multiple_of(group * local, local)
        part = by_height[pl.ds(start, local), :]
        depth_out[0, side, :local] = part
        depth_out[0, side, local:] = zeros
        depth_out[1, side, :pad] = zeros
        depth_out[1, side, pad:] = part
        synth_out[side * local : (side + 1) * local] = turned[pl.ds(start, local), :]


def vertical(own, depth_analysis, synthesis, *after, micros=0):
    fields, total, _ = depth_analysis.shape
    square = pl.BlockSpec((None, total, total), lambda i, *_: (i, 0, 0))
    return pl.pallas_call(
        vertical_kernel,
        grid_spec=pltpu.PrefetchScalarGridSpec(
            num_scalar_prefetch=1,
            grid=(fields,),
            in_specs=[square, square, *([pl.BlockSpec(memory_space=pl.ANY)] * len(after))],
            out_specs=[
                pl.BlockSpec((None, 2, 2, 256, total), lambda i, *_: (i, 0, 0, 0, 0)),
                square,
            ],
            scratch_shapes=[pltpu.VMEM((total, total), BF16)] * 2,
        ),
        out_shape=[
            jax.ShapeDtypeStruct((fields, 2, 2, 256, total), BF16),
            jax.ShapeDtypeStruct((fields, total, total), BF16),
        ],
        compiler_params=params(62),
        cost_estimate=cost(micros),
        name="vertical",
    )(own, depth_analysis, synthesis, *after)


def solve_kernel(first, part, place_ref, modes_ref, *rest):
    x, table_ref, depth_ref, synth_ref, tau_ref, step_ref = rest[:6]
    own_ref, other_ref, spread = rest[-3:]
    sources, _, some, radii, lanes = x.shape
    modes_here = table_ref.shape[2]
    half = synth_ref.shape[0] // 2
    quarter = half // 2
    near = 1 - place_ref[0]
    step = step_ref[0, 0]
    block = first + pl.program_id(0)
    n_index = lax.broadcasted_iota(jnp.int32, (modes_here, 1), 0) + block * modes_here
    tau = 1.0 + step * tau_ref[...]
    for q in range(some):
        projected = [None, None]
        for g, parts in enumerate((((0, 3), (1, 2)), ((near, 0), (1 - near, 1)))):
            radial = sum(
                dot(table_ref[q, side], x[:, at, q].reshape(sources * radii, lanes), NN)
                for side, at in parts
            ).astype(BF16)
            for p in range(2):
                term = dot(radial[:, p * 128 : p * 128 + 256], depth_ref[p, g], NN)
                projected[p] = term if g == 0 else projected[p] + term
        summed = modes_ref[q + (some if part == 1 else 0)] + 2 * n_index
        weight = (summed * (summed + 2)).astype(F32) * (step / float(512 * 512))
        scale = 1.0 / (weight + tau)
        for p in range(2):
            eigen = (projected[p] * scale).astype(BF16)
            found = dot(synth_ref[...], eigen, NT)
            at = 2 * q + p
            if part is None:
                spread[:, at, :] = found
                continue
            if part == 0:
                spread[:quarter, at, :] = found[:quarter]
                spread[:quarter, 4 + at, :] = found[quarter:half]
            else:
                spread[:half, 4 + at, :] = found[:half]
            spread[half : half + quarter, at, :] = found[half : half + quarter]
            spread[half : half + quarter, 4 + at, :] = found[half + quarter :]
    if part is None:
        own_ref[...] = spread[:half].astype(BF16)
        other_ref[...] = spread[half:].astype(BF16)
        return
    if part == 0:
        own_ref[...] = spread[:quarter].astype(BF16)
    else:
        early = rest[6][...].astype(F32)
        low, high = side_by_side(early, spread[:quarter], spread[quarter:half])
        own_ref[:quarter] = low.astype(BF16)
        own_ref[quarter:] = high.astype(BF16)
    other_ref[...] = spread[half : half + quarter].astype(BF16)


def side_by_side(early, low, high):
    row = lax.broadcasted_iota(jnp.int32, early.shape, 1)
    return jnp.where(row < 4, early, low), jnp.where(row < 4, pltpu.roll(early, 4, axis=1), high)


def solve(place, modes, x, table, depth, synth, tau, steps, field, out, blocks, *after, part=None, early=None, micros=0):
    depth_total = synth.shape[1]
    some, radial_size = x.shape[2], table.shape[2]
    half, cols = depth_total // 2, 8
    fields = synth.shape[0]
    block = 256
    first, count = blocks
    const = lambda shape: pl.BlockSpec(shape, lambda i, *_: (0,) * len(shape))
    of_field = lambda *shape: pl.BlockSpec((None, *shape), lambda i, *_: (field,) + (0,) * len(shape))
    slots_at = 1 if part == 1 else 0
    in_specs = [
        const(x.shape),
        pl.BlockSpec((some, 2, block, table.shape[3]), lambda i, *_: (slots_at, 0, first + i, 0)),
        of_field(*depth.shape[1:]),
        of_field(depth_total, depth_total),
        of_field(1, depth_total),
        of_field(1, 1),
    ]
    args = [place, modes, x, table, depth, synth, tau[:, None, :], steps[:, None, None]]
    packed = (half // 2, cols, block)
    if part == 1:
        in_specs.append(pl.BlockSpec(packed, lambda i, *_: (0, 0, first + i)))
        args.append(early)
    aliases = {}
    if out is not None:
        in_specs.append(pl.BlockSpec(memory_space=pl.ANY))
        args.append(out)
        aliases = {len(args) - 1: 0}
    in_specs += [pl.BlockSpec(memory_space=pl.ANY)] * len(after)
    args += after
    height = half if part is None else half // 2
    if part == 0:
        own_spec = pl.BlockSpec(packed, lambda i, *_: (0, 0, i))
        own_shape = (half // 2, cols, count * block)
    else:
        own_spec = pl.BlockSpec(
            (half, None, cols, block), lambda i, place, _: (0, field, place[0], first + i)
        )
        own_shape = (half, fields, 2 * cols, radial_size)
    return pl.pallas_call(
        functools.partial(solve_kernel, first, part),
        grid_spec=pltpu.PrefetchScalarGridSpec(
            num_scalar_prefetch=2,
            grid=(count,),
            in_specs=in_specs,
            out_specs=[own_spec, pl.BlockSpec((height, cols, block), lambda i, *_: (0, 0, i))],
            scratch_shapes=[pltpu.VMEM((depth_total, cols, block), F32)],
        ),
        out_shape=[
            jax.ShapeDtypeStruct(own_shape, BF16),
            jax.ShapeDtypeStruct((height, cols, count * block), BF16),
        ],
        input_output_aliases=aliases,
        compiler_params=params(62),
        cost_estimate=cost(micros),
        name="solve",
    )(*args)


def merge_kernel(place_ref, early_ref, late_ref, _, out_ref):
    quarter = early_ref.shape[0]
    late = late_ref[...].astype(F32)
    low, high = side_by_side(early_ref[...].astype(F32), pltpu.roll(late, 4, axis=1), late)
    out_ref[:quarter] = low.astype(BF16)
    out_ref[quarter:] = high.astype(BF16)


def merge(place, early, late, field, first, out, micros):
    packed = late.shape
    quarter, cols, block = packed
    return pl.pallas_call(
        merge_kernel,
        grid_spec=pltpu.PrefetchScalarGridSpec(
            num_scalar_prefetch=1,
            grid=(1,),
            in_specs=[
                pl.BlockSpec(packed, lambda i, _: (0, 0, first)),
                pl.BlockSpec(packed, lambda i, _: (0, 0, 0)),
                pl.BlockSpec(memory_space=pl.ANY),
            ],
            out_specs=pl.BlockSpec(
                (2 * quarter, None, cols, block), lambda i, place: (0, field, 1 - place[0], first)
            ),
        ),
        out_shape=jax.ShapeDtypeStruct(out.shape, BF16),
        input_output_aliases={3: 0},
        compiler_params=params(62),
        cost_estimate=cost(micros),
        name="merge",
    )(place, early, late, out)


def place_kernel(place_ref, received_ref, _, out_ref):
    out_ref[...] = received_ref[...]


def put(place, received, field, first, out, micros):
    half, cols, radial_size = received.shape
    return pl.pallas_call(
        place_kernel,
        grid_spec=pltpu.PrefetchScalarGridSpec(
            num_scalar_prefetch=1,
            grid=(1,),
            in_specs=[
                pl.BlockSpec((half, cols, radial_size), lambda i, _: (i, 0, 0)),
                pl.BlockSpec(memory_space=pl.ANY),
            ],
            out_specs=pl.BlockSpec(
                (half, None, cols, radial_size), lambda i, place: (i, field, 1 - place[0], first)
            ),
        ),
        out_shape=jax.ShapeDtypeStruct(out.shape, BF16),
        input_output_aliases={2: 0},
        compiler_params=params(62),
        cost_estimate=cost(micros),
        name="put",
    )(place, received, out)


def shards(
    fields,
    radial_tables,
    radial_counts,
    assignment,
    depth_analysis,
    synthesis,
    tau_values,
    time_steps,
):
    depth_local, field_count, radii, grid_size = fields.shape
    depth_total = depth_analysis.shape[1]
    mode_count = grid_size // 2
    block_count = assignment.shape[0]
    block_size = mode_count // block_count
    group, upper = lax.axis_index("xl"), lax.axis_index("xh")
    ring = lax.axis_index(("z", "y", "xh", "core"))
    place = group[None].astype(jnp.int32)
    inner = jnp.arange(block_size, dtype=jnp.int32)

    by_x = assignment.reshape(16, 2, 2, 2).transpose(1, 3, 0, 2).reshape(4, 32)
    by_x = lax.dynamic_slice_in_dim(jnp.concatenate([by_x, by_x]), 2 * upper + group, 4)
    ordered = jnp.stack([by_x[shift] for shift in SHIFTS])
    modes_to = ordered[None, :, :, None] * block_size + inner.reshape(2, 1, 1, 2)
    modes_to = modes_to.reshape(mode_count)
    phase = phase_rows(modes_to, grid_size)
    index = jnp.arange(256, dtype=jnp.int32)
    heights = 256 // radii
    origin = (index % heights) * radii + index // heights
    swap = (origin[:, None] == index[None, :]).astype(BF16)

    def along_x(pieces):
        return [along(x, shift) for x, shift in zip(pieces, SHIFTS[:3], strict=True)]

    def across(x):
        return lax.all_to_all(x, ("z", "y", "core"), 0, 0, tiled=True)

    def solved(x, field, out, blocks, *after, **options):
        operands = (table, depth, synth, tau_values, time_steps, field, out, blocks)
        out, other = solve(place, modes_here, x, *operands, *after, **options)
        return out, lax.ppermute(other, "xl", [(0, 1), (1, 0)])

    def sent_of(field, halves, *after, **options):
        *moving, own = azimuth(phase, swap, fields, field, halves, *after, **options)
        return [*along_x(moving), own]

    whole, low_n, high_n = (0, 2), (0, 1), (1, 1)
    a = sent_of(0, (0, 1))
    b = sent_of(1, whole, a[3], micros=COSTS["azB"])
    a = join(a, b[3], micros=COSTS["joinA"])
    c = sent_of(2, whole, a, micros=COSTS["azC"])
    a = across(a)
    b = join(b, c[3], micros=COSTS["joinB"])

    own = jnp.stack([group, upper]).astype(jnp.int32)
    own_block = lax.dynamic_slice_in_dim(assignment, ring * 2 + group, 1)
    modes_here = own_block * block_size + inner
    depth, synth = vertical(own, depth_analysis, synthesis, b, micros=COSTS["vertical"])
    d = sent_of(0, (1, 1), depth, micros=COSTS["azD"])
    table = tables(own, modes_here, radial_counts, radial_tables, radii, d[3], micros=COSTS["tables"])

    b = across(b)
    c = join(c, table, depth, synth, micros=COSTS["joinC"])
    early, other_a = solved(a, 0, None, whole, c, part=0, micros=COSTS["sA"])
    c = across(c)
    out, other1a = solved(b, 1, None, low_n, early, micros=COSTS["s1a"])
    out, other1b = solved(b, 1, out, high_n, micros=COSTS["s1b"])
    d = across(join(d, out, micros=COSTS["joinD"]))
    out = put(place, other1a, 1, 0, out, micros=COSTS["p1a"])
    out, other2a = solved(c, 2, out, low_n, other_a, micros=COSTS["s2a"])
    out = put(place, other1b, 1, 1, out, micros=COSTS["p1b"])
    out, other2b = solved(c, 2, out, high_n, micros=COSTS["s2b"])
    out, other_da = solved(d, 0, out, low_n, part=1, early=early, micros=COSTS["sDa"])
    out = put(place, other2a, 2, 0, out, micros=COSTS["p2a"])
    out, other_db = solved(d, 0, out, high_n, part=1, early=early, micros=COSTS["sDb"])
    out = put(place, other2b, 2, 1, out, micros=COSTS["p2b"])
    out = merge(place, other_a, other_da, 0, 0, out, micros=COSTS["mDa"])
    return merge(place, other_a, other_db, 0, 1, out, micros=COSTS["mDb"])


def solution(mesh):
    split = Mesh(mesh.devices.reshape(2, 4, 4, 2, 2), ("xl", "z", "y", "xh", "core"))
    ma = ("z", "y", "xh", "core")
    placed = (P("xl", None, ma, None), P(ma, None, None), P(), P(), P(), P(), P(), P())
    return jax.shard_map(
        shards, mesh=split, in_specs=placed, out_specs=P("xl", None, ma, None), check_vma=False
    )
```

```python
import functools
import math

import jax
import jax.numpy as jnp
from jax import lax
from jax.experimental import pallas as pl
from jax.experimental.pallas import tpu as pltpu
from jax.sharding import Mesh
from jax.sharding import PartitionSpec as P

F32, BF16 = jnp.float32, jnp.bfloat16
NT = (((1,), (1,)), ((), ()))
NN = (((1,), (0,)), ((), ()))
MIB = 1 << 20


def cost(micros):
    return pl.CostEstimate(flops=micros * 10**9, bytes_accessed=1000, transcendentals=0)


COSTS = {'vertical': 80, 'tables': 0, 'azB': 0, 'azC': 20, 'azD': 0, 'joinA': 0, 'joinB': 20, 'joinC': 0, 'joinD': 5, 'sA': 0, 's1a': 0, 's1b': 40, 's2a': 0, 's2b': 0, 'sDa': 0, 'sDb': 0, 'p1a': 1, 'p1b': 1, 'p2a': 30, 'p2b': 1, 'mDa': 1, 'mDb': 1}
SHORT = cost(0)
SHIFTS = (1, 3, 2, 0)


def along(x, shift):
    at = lambda chip: (chip % 2) * 2 + chip // 2
    return lax.ppermute(x, ("xl", "xh"), [(at(i), at((i + shift) % 4)) for i in range(4)])


def dot(a, b, dims):
    return lax.dot_general(a, b, dims, preferred_element_type=F32)


def params(mib):
    return pltpu.CompilerParams(vmem_limit_bytes=mib * MIB)


def phase_kernel(c0_ref, s0_ref, c1_ref, s1_ref, out_ref):
    c0, s0 = c0_ref[...], s0_ref[...]
    width = c0.shape[1]
    for block in range(out_ref.shape[2] // width):
        c1, s1 = c1_ref[:, block : block + 1], s1_ref[:, block : block + 1]
        lanes = slice(block * width, (block + 1) * width)
        out_ref[0, :, lanes] = (c0 * c1 - s0 * s1).astype(BF16)
        out_ref[1, :, lanes] = -(s0 * c1 + c0 * s1).astype(BF16)


def phase_rows(modes, grid_size):
    width = 128

    def tables(points, scale):
        index = (modes[:, None] * points[None, :]) % grid_size
        angle = index.astype(F32) * (2.0 * math.pi / grid_size)
        return jnp.cos(angle) * scale, jnp.sin(angle) * scale

    c0, s0 = tables(jnp.arange(width, dtype=jnp.int32), math.sqrt(2.0 / grid_size))
    c1, s1 = tables(jnp.arange(grid_size // width, dtype=jnp.int32) * width, 1.0)
    return pl.pallas_call(
        phase_kernel,
        out_shape=jax.ShapeDtypeStruct((2, modes.shape[0], grid_size), BF16),
        compiler_params=params(40),
        cost_estimate=SHORT,
        name="phase_table",
    )(c0, s0, c1, s1)


def azimuth_kernel(many, phase_ref, swap_ref, x_ref, *rest):
    outs, (rows, spread) = rest[many:-2], rest[-2:]
    depth, radii, grid_size = x_ref.shape
    pad = 256 - depth
    group = 256 // radii

    @pl.when(pl.program_id(0) == 0)
    def _():
        zeros = jnp.zeros((pad, grid_size), BF16)
        for r in range(radii):
            rows[r, 0:pad] = zeros
            rows[r, pad + depth :] = zeros
        for block in range(depth // group):
            heights = slice(block * group, (block + 1) * group)
            swapped = dot(swap_ref[...], x_ref[heights].reshape(256, grid_size), NN).astype(BF16)
            for r in range(radii):
                start = pad + block * group
                rows[r, start : start + group] = swapped[r * group : (r + 1) * group]

    for r in range(radii):
        cosine = dot(phase_ref[0], rows[r, pad:], NT)
        sine = dot(phase_ref[1], rows[r, 0:256], NT)
        spread[:, r, 0:128] = cosine[:, :128]
        spread[:, r, 128:256] = cosine[:, 128:] + sine[:, :128]
        spread[:, r, 256:384] = sine[:, 128:]
    count = spread.shape[0] // len(outs)
    for j, out in enumerate(outs):
        piece = spread[j * count : (j + 1) * count].astype(BF16)
        out[...] = piece.reshape(out.shape)


def azimuth(phase, swap, fields, field, halves, *after, micros=0):
    depth, _, radii, grid_size = fields.shape
    first, count = halves
    rows = phase.shape[1] // 2
    piece = (rows // 8, 2, radii, 2 * depth)
    whole = lambda shape: pl.BlockSpec(shape, lambda i: (0,) * len(shape))
    return pl.pallas_call(
        functools.partial(azimuth_kernel, len(after)),
        grid=(count,),
        in_specs=[
            pl.BlockSpec((2, rows, grid_size), lambda i: (0, first + i, 0)),
            whole(swap.shape),
            pl.BlockSpec((depth, None, radii, grid_size), lambda i: (0, field, 0, 0)),
            *([pl.BlockSpec(memory_space=pl.ANY)] * len(after)),
        ],
        out_specs=[pl.BlockSpec(piece, lambda i: (0, i, 0, 0))] * 4,
        out_shape=[jax.ShapeDtypeStruct((piece[0], 2 * count, *piece[2:]), BF16)] * 4,
        scratch_shapes=[
            pltpu.VMEM((radii, 512 - depth, grid_size), BF16),
            pltpu.VMEM((rows, radii, 2 * depth), F32),
        ],
        compiler_params=params(48),
        cost_estimate=cost(micros),
        name="azimuth",
    )(phase, swap, fields, *after)


def join_kernel(*refs):
    for at, piece in enumerate(refs[:4]):
        refs[-1][:, at] = piece[...]


def join(pieces, *after, micros=0):
    steps = 2
    shape = pieces[0].shape
    block = (shape[0] // steps, *shape[1:])
    return pl.pallas_call(
        join_kernel,
        grid=(steps,),
        in_specs=[pl.BlockSpec(block, lambda i: (i, 0, 0, 0))] * 4
        + [pl.BlockSpec(memory_space=pl.ANY)] * len(after),
        out_specs=pl.BlockSpec((block[0], 4, *block[1:]), lambda i: (i, 0, 0, 0, 0)),
        out_shape=jax.ShapeDtypeStruct((shape[0], 4, *shape[1:]), BF16),
        compiler_params=params(62),
        cost_estimate=cost(micros),
        name="join",
    )(*pieces, *after)


def tables_kernel(own_ref, modes_ref, counts_ref, table_ref, *rest):
    out_ref = rest[-1]
    rows, size = out_ref.shape[1:]
    kept = counts_ref[modes_ref[pl.program_id(0)]]
    n_index = lax.broadcasted_iota(jnp.int32, (rows, 1), 0)
    for side in range(2):
        upper = own_ref[1] if side == 0 else 1 - own_ref[1]
        part = table_ref[:, upper].astype(F32).reshape(size, rows)
        out_ref[side] = jnp.where(n_index < kept, part.T, 0.0).astype(BF16)


def tables(own, modes, counts, radial_tables, radii, *after, micros=0):
    slots, radial_total, radial_size = radial_tables.shape
    slots //= 2
    split = (16, 2, 2, radii, radial_size)
    return pl.pallas_call(
        tables_kernel,
        grid_spec=pltpu.PrefetchScalarGridSpec(
            num_scalar_prefetch=3,
            grid=(slots,),
            in_specs=[
                pl.BlockSpec((None, *split), lambda i, own, *_: (own[0] * slots + i, 0, 0, 0, 0, 0)),
                *([pl.BlockSpec(memory_space=pl.ANY)] * len(after)),
            ],
            out_specs=pl.BlockSpec(
                (None, 2, radial_size, radial_total // 2), lambda i, *_: (i, 0, 0, 0)
            ),
        ),
        out_shape=jax.ShapeDtypeStruct((slots, 2, radial_size, radial_total // 2), BF16),
        compiler_params=params(62),
        cost_estimate=cost(micros),
        name="tables",
    )(own, modes, counts, radial_tables.reshape(2 * slots, *split), *after)


def vertical_kernel(own_ref, depth_ref, synth_ref, *rest):
    by_height, turned, depth_out, synth_out = rest[-1], rest[-2], rest[-4], rest[-3]
    local = synth_ref.shape[0] // 2
    pad = 256 - local
    by_height[...] = depth_ref[...].astype(F32).T.astype(BF16)
    turned[...] = synth_ref[...]
    zeros = jnp.zeros((pad, synth_ref.shape[0]), BF16)
    for side in range(2):
        group = own_ref[0] if side == 0 else 1 - own_ref[0]
        start = pl.multiple_of(group * local, local)
        part = by_height[pl.ds(start, local), :]
        depth_out[0, side, :local] = part
        depth_out[0, side, local:] = zeros
        depth_out[1, side, :pad] = zeros
        depth_out[1, side, pad:] = part
        synth_out[side * local : (side + 1) * local] = turned[pl.ds(start, local), :]


def vertical(own, depth_analysis, synthesis, *after, micros=0):
    fields, total, _ = depth_analysis.shape
    square = pl.BlockSpec((None, total, total), lambda i, *_: (i, 0, 0))
    return pl.pallas_call(
        vertical_kernel,
        grid_spec=pltpu.PrefetchScalarGridSpec(
            num_scalar_prefetch=1,
            grid=(fields,),
            in_specs=[square, square, *([pl.BlockSpec(memory_space=pl.ANY)] * len(after))],
            out_specs=[
                pl.BlockSpec((None, 2, 2, 256, total), lambda i, *_: (i, 0, 0, 0, 0)),
                square,
            ],
            scratch_shapes=[pltpu.VMEM((total, total), BF16)] * 2,
        ),
        out_shape=[
            jax.ShapeDtypeStruct((fields, 2, 2, 256, total), BF16),
            jax.ShapeDtypeStruct((fields, total, total), BF16),
        ],
        compiler_params=params(62),
        cost_estimate=cost(micros),
        name="vertical",
    )(own, depth_analysis, synthesis, *after)


def solve_kernel(first, part, place_ref, modes_ref, *rest):
    x, table_ref, depth_ref, synth_ref, tau_ref, step_ref = rest[:6]
    own_ref, other_ref, spread = rest[-3:]
    sources, _, some, radii, lanes = x.shape
    modes_here = table_ref.shape[2]
    half = synth_ref.shape[0] // 2
    quarter = half // 2
    near = 1 - place_ref[0]
    step = step_ref[0, 0]
    block = first + pl.program_id(0)
    n_index = lax.broadcasted_iota(jnp.int32, (modes_here, 1), 0) + block * modes_here
    tau = 1.0 + step * tau_ref[...]
    for q in range(some):
        projected = [None, None]
        for g, parts in enumerate((((0, 3), (1, 2)), ((near, 0), (1 - near, 1)))):
            radial = sum(
                dot(table_ref[q, side], x[:, at, q].reshape(sources * radii, lanes), NN)
                for side, at in parts
            ).astype(BF16)
            for p in range(2):
                term = dot(radial[:, p * 128 : p * 128 + 256], depth_ref[p, g], NN)
                projected[p] = term if g == 0 else projected[p] + term
        summed = modes_ref[q + (some if part == 1 else 0)] + 2 * n_index
        weight = (summed * (summed + 2)).astype(F32) * (step / float(512 * 512))
        scale = 1.0 / (weight + tau)
        for p in range(2):
            eigen = (projected[p] * scale).astype(BF16)
            found = dot(synth_ref[...], eigen, NT)
            at = 2 * q + p
            if part is None:
                spread[:, at, :] = found
                continue
            if part == 0:
                spread[:quarter, at, :] = found[:quarter]
                spread[:quarter, 4 + at, :] = found[quarter:half]
            else:
                spread[:half, 4 + at, :] = found[:half]
            spread[half : half + quarter, at, :] = found[half : half + quarter]
            spread[half : half + quarter, 4 + at, :] = found[half + quarter :]
    if part is None:
        own_ref[...] = spread[:half].astype(BF16)
        other_ref[...] = spread[half:].astype(BF16)
        return
    if part == 0:
        own_ref[...] = spread[:quarter].astype(BF16)
    else:
        early = rest[6][...].astype(F32)
        low, high = side_by_side(early, spread[:quarter], spread[quarter:half])
        own_ref[:quarter] = low.astype(BF16)
        own_ref[quarter:] = high.astype(BF16)
    other_ref[...] = spread[half : half + quarter].astype(BF16)


def side_by_side(early, low, high):
    row = lax.broadcasted_iota(jnp.int32, early.shape, 1)
    return jnp.where(row < 4, early, low), jnp.where(row < 4, pltpu.roll(early, 4, axis=1), high)


def solve(place, modes, x, table, depth, synth, tau, steps, field, out, blocks, *after, part=None, early=None, micros=0):
    depth_total = synth.shape[1]
    some, radial_size = x.shape[2], table.shape[2]
    half, cols = depth_total // 2, 8
    fields = synth.shape[0]
    block = 256
    first, count = blocks
    const = lambda shape: pl.BlockSpec(shape, lambda i, *_: (0,) * len(shape))
    of_field = lambda *shape: pl.BlockSpec((None, *shape), lambda i, *_: (field,) + (0,) * len(shape))
    slots_at = 1 if part == 1 else 0
    in_specs = [
        const(x.shape),
        pl.BlockSpec((some, 2, block, table.shape[3]), lambda i, *_: (slots_at, 0, first + i, 0)),
        of_field(*depth.shape[1:]),
        of_field(depth_total, depth_total),
        of_field(1, depth_total),
        of_field(1, 1),
    ]
    args = [place, modes, x, table, depth, synth, tau[:, None, :], steps[:, None, None]]
    packed = (half // 2, cols, block)
    if part == 1:
        in_specs.append(pl.BlockSpec(packed, lambda i, *_: (0, 0, first + i)))
        args.append(early)
    aliases = {}
    if out is not None:
        in_specs.append(pl.BlockSpec(memory_space=pl.ANY))
        args.append(out)
        aliases = {len(args) - 1: 0}
    in_specs += [pl.BlockSpec(memory_space=pl.ANY)] * len(after)
    args += after
    height = half if part is None else half // 2
    if part == 0:
        own_spec = pl.BlockSpec(packed, lambda i, *_: (0, 0, i))
        own_shape = (half // 2, cols, count * block)
    else:
        own_spec = pl.BlockSpec(
            (half, None, cols, block), lambda i, place, _: (0, field, place[0], first + i)
        )
        own_shape = (half, fields, 2 * cols, radial_size)
    return pl.pallas_call(
        functools.partial(solve_kernel, first, part),
        grid_spec=pltpu.PrefetchScalarGridSpec(
            num_scalar_prefetch=2,
            grid=(count,),
            in_specs=in_specs,
            out_specs=[own_spec, pl.BlockSpec((height, cols, block), lambda i, *_: (0, 0, i))],
            scratch_shapes=[pltpu.VMEM((depth_total, cols, block), F32)],
        ),
        out_shape=[
            jax.ShapeDtypeStruct(own_shape, BF16),
            jax.ShapeDtypeStruct((height, cols, count * block), BF16),
        ],
        input_output_aliases=aliases,
        compiler_params=params(62),
        cost_estimate=cost(micros),
        name="solve",
    )(*args)


def merge_kernel(place_ref, early_ref, late_ref, _, out_ref):
    quarter = early_ref.shape[0]
    late = late_ref[...].astype(F32)
    low, high = side_by_side(early_ref[...].astype(F32), pltpu.roll(late, 4, axis=1), late)
    out_ref[:quarter] = low.astype(BF16)
    out_ref[quarter:] = high.astype(BF16)


def merge(place, early, late, field, first, out, micros):
    packed = late.shape
    quarter, cols, block = packed
    return pl.pallas_call(
        merge_kernel,
        grid_spec=pltpu.PrefetchScalarGridSpec(
            num_scalar_prefetch=1,
            grid=(1,),
            in_specs=[
                pl.BlockSpec(packed, lambda i, _: (0, 0, first)),
                pl.BlockSpec(packed, lambda i, _: (0, 0, 0)),
                pl.BlockSpec(memory_space=pl.ANY),
            ],
            out_specs=pl.BlockSpec(
                (2 * quarter, None, cols, block), lambda i, place: (0, field, 1 - place[0], first)
            ),
        ),
        out_shape=jax.ShapeDtypeStruct(out.shape, BF16),
        input_output_aliases={3: 0},
        compiler_params=params(24),
        cost_estimate=cost(micros),
        name="merge",
    )(place, early, late, out)


def place_kernel(place_ref, received_ref, _, out_ref):
    out_ref[...] = received_ref[...]


def put(place, received, field, first, out, micros):
    half, cols, radial_size = received.shape
    return pl.pallas_call(
        place_kernel,
        grid_spec=pltpu.PrefetchScalarGridSpec(
            num_scalar_prefetch=1,
            grid=(1,),
            in_specs=[
                pl.BlockSpec((half, cols, radial_size), lambda i, _: (i, 0, 0)),
                pl.BlockSpec(memory_space=pl.ANY),
            ],
            out_specs=pl.BlockSpec(
                (half, None, cols, radial_size), lambda i, place: (i, field, 1 - place[0], first)
            ),
        ),
        out_shape=jax.ShapeDtypeStruct(out.shape, BF16),
        input_output_aliases={2: 0},
        compiler_params=params(24),
        cost_estimate=cost(micros),
        name="put",
    )(place, received, out)


def shards(
    fields,
    radial_tables,
    radial_counts,
    assignment,
    depth_analysis,
    synthesis,
    tau_values,
    time_steps,
):
    depth_local, field_count, radii, grid_size = fields.shape
    depth_total = depth_analysis.shape[1]
    mode_count = grid_size // 2
    block_count = assignment.shape[0]
    block_size = mode_count // block_count
    group, upper = lax.axis_index("xl"), lax.axis_index("xh")
    ring = lax.axis_index(("z", "y", "xh", "core"))
    place = group[None].astype(jnp.int32)
    inner = jnp.arange(block_size, dtype=jnp.int32)

    by_x = assignment.reshape(16, 2, 2, 2).transpose(1, 3, 0, 2).reshape(4, 32)
    by_x = lax.dynamic_slice_in_dim(jnp.concatenate([by_x, by_x]), 2 * upper + group, 4)
    ordered = jnp.stack([by_x[shift] for shift in SHIFTS])
    modes_to = ordered[None, :, :, None] * block_size + inner.reshape(2, 1, 1, 2)
    modes_to = modes_to.reshape(mode_count)
    phase = phase_rows(modes_to, grid_size)
    index = jnp.arange(256, dtype=jnp.int32)
    heights = 256 // radii
    origin = (index % heights) * radii + index // heights
    swap = (origin[:, None] == index[None, :]).astype(BF16)

    def along_x(pieces):
        return [along(x, shift) for x, shift in zip(pieces, SHIFTS[:3], strict=True)]

    def across(x):
        return lax.all_to_all(x, ("z", "y", "core"), 0, 0, tiled=True)

    def solved(x, field, out, blocks, *after, **options):
        operands = (table, depth, synth, tau_values, time_steps, field, out, blocks)
        out, other = solve(place, modes_here, x, *operands, *after, **options)
        return out, lax.ppermute(other, "xl", [(0, 1), (1, 0)])

    def sent_of(field, halves, *after, **options):
        *moving, own = azimuth(phase, swap, fields, field, halves, *after, **options)
        return [*along_x(moving), own]

    whole, low_n, high_n = (0, 2), (0, 1), (1, 1)
    a = sent_of(0, (0, 1))
    b = sent_of(1, whole, a[3], micros=COSTS["azB"])
    a = join(a, b[3], micros=COSTS["joinA"])
    c = sent_of(2, whole, a, micros=COSTS["azC"])
    a = across(a)
    b = join(b, c[3], micros=COSTS["joinB"])

    own = jnp.stack([group, upper]).astype(jnp.int32)
    own_block = lax.dynamic_slice_in_dim(assignment, ring * 2 + group, 1)
    modes_here = own_block * block_size + inner
    depth, synth = vertical(own, depth_analysis, synthesis, b, micros=COSTS["vertical"])
    d = sent_of(0, (1, 1), depth, micros=COSTS["azD"])
    table = tables(own, modes_here, radial_counts, radial_tables, radii, d[3], micros=COSTS["tables"])

    b = across(b)
    c = join(c, table, depth, synth, micros=COSTS["joinC"])
    early, other_a = solved(a, 0, None, whole, c, part=0, micros=COSTS["sA"])
    c = across(c)
    out, other1a = solved(b, 1, None, low_n, early, micros=COSTS["s1a"])
    out, other1b = solved(b, 1, out, high_n, micros=COSTS["s1b"])
    out, other2a = solved(c, 2, out, low_n, other_a, micros=COSTS["s2a"])
    d = across(join(d, out, micros=COSTS["joinD"]))
    out, other2b = solved(c, 2, out, high_n, micros=COSTS["s2b"])
    out = put(place, other1a, 1, 0, out, micros=COSTS["p1a"])
    out = put(place, other1b, 1, 1, out, micros=COSTS["p1b"])
    out = put(place, other2a, 2, 0, out, micros=COSTS["p2a"])
    out, other_da = solved(d, 0, out, low_n, part=1, early=early, micros=COSTS["sDa"])
    out, other_db = solved(d, 0, out, high_n, part=1, early=early, micros=COSTS["sDb"])
    out = put(place, other2b, 2, 1, out, micros=COSTS["p2b"])
    out = merge(place, other_a, other_da, 0, 0, out, micros=COSTS["mDa"])
    return merge(place, other_a, other_db, 0, 1, out, micros=COSTS["mDb"])


def solution(mesh):
    split = Mesh(mesh.devices.reshape(2, 4, 4, 2, 2), ("xl", "z", "y", "xh", "core"))
    ma = ("z", "y", "xh", "core")
    placed = (P("xl", None, ma, None), P(ma, None, None), P(), P(), P(), P(), P(), P())
    return jax.shard_map(
        shards, mesh=split, in_specs=placed, out_specs=P("xl", None, ma, None), check_vma=False
    )
```

```python
import functools
import math

import jax
import jax.numpy as jnp
from jax import lax
from jax.experimental import pallas as pl
from jax.experimental.pallas import tpu as pltpu
from jax.sharding import Mesh
from jax.sharding import PartitionSpec as P

F32, BF16 = jnp.float32, jnp.bfloat16
NT = (((1,), (1,)), ((), ()))
NN = (((1,), (0,)), ((), ()))
MIB = 1 << 20


def cost(micros):
    return pl.CostEstimate(flops=micros * 10**9, bytes_accessed=1000, transcendentals=0)


COSTS = {'tie': 0, 'vertical': 80, 'tables': 0, 'azB': 0, 'azC': 20, 'azD': 0, 'joinA': 0, 'joinB': 20, 'joinC': 0, 'joinD': 0, 'sA': 0, 's1a': 0, 's1b': 40, 's2a': 0, 's2b': 0, 'sDa': 0, 'sDb': 0, 'p1a': 1, 'p1b': 1, 'p2a': 30, 'p2b': 1, 'mDa': 1, 'mDb': 1}
SHORT = cost(0)
SHIFTS = (1, 3, 2, 0)


def along(x, shift):
    at = lambda chip: (chip % 2) * 2 + chip // 2
    return lax.ppermute(x, ("xl", "xh"), [(at(i), at((i + shift) % 4)) for i in range(4)])


def dot(a, b, dims):
    return lax.dot_general(a, b, dims, preferred_element_type=F32)


def params(mib):
    return pltpu.CompilerParams(vmem_limit_bytes=mib * MIB)


def phase_kernel(c0_ref, s0_ref, c1_ref, s1_ref, out_ref):
    c0, s0 = c0_ref[...], s0_ref[...]
    width = c0.shape[1]
    for block in range(out_ref.shape[2] // width):
        c1, s1 = c1_ref[:, block : block + 1], s1_ref[:, block : block + 1]
        lanes = slice(block * width, (block + 1) * width)
        out_ref[0, :, lanes] = (c0 * c1 - s0 * s1).astype(BF16)
        out_ref[1, :, lanes] = -(s0 * c1 + c0 * s1).astype(BF16)


def phase_rows(modes, grid_size):
    width = 128

    def tables(points, scale):
        index = (modes[:, None] * points[None, :]) % grid_size
        angle = index.astype(F32) * (2.0 * math.pi / grid_size)
        return jnp.cos(angle) * scale, jnp.sin(angle) * scale

    c0, s0 = tables(jnp.arange(width, dtype=jnp.int32), math.sqrt(2.0 / grid_size))
    c1, s1 = tables(jnp.arange(grid_size // width, dtype=jnp.int32) * width, 1.0)
    return pl.pallas_call(
        phase_kernel,
        out_shape=jax.ShapeDtypeStruct((2, modes.shape[0], grid_size), BF16),
        compiler_params=params(40),
        cost_estimate=SHORT,
        name="phase_table",
    )(c0, s0, c1, s1)


def azimuth_kernel(many, phase_ref, swap_ref, x_ref, *rest):
    outs, (rows, spread) = rest[many:-2], rest[-2:]
    depth, radii, grid_size = x_ref.shape
    pad = 256 - depth
    group = 256 // radii

    @pl.when(pl.program_id(0) == 0)
    def _():
        zeros = jnp.zeros((pad, grid_size), BF16)
        for r in range(radii):
            rows[r, 0:pad] = zeros
            rows[r, pad + depth :] = zeros
        for block in range(depth // group):
            heights = slice(block * group, (block + 1) * group)
            swapped = dot(swap_ref[...], x_ref[heights].reshape(256, grid_size), NN).astype(BF16)
            for r in range(radii):
                start = pad + block * group
                rows[r, start : start + group] = swapped[r * group : (r + 1) * group]

    for r in range(radii):
        cosine = dot(phase_ref[0], rows[r, pad:], NT)
        sine = dot(phase_ref[1], rows[r, 0:256], NT)
        spread[:, r, 0:128] = cosine[:, :128]
        spread[:, r, 128:256] = cosine[:, 128:] + sine[:, :128]
        spread[:, r, 256:384] = sine[:, 128:]
    count = spread.shape[0] // len(outs)
    for j, out in enumerate(outs):
        piece = spread[j * count : (j + 1) * count].astype(BF16)
        out[...] = piece.reshape(out.shape)


def azimuth(phase, swap, fields, field, halves, *after, micros=0):
    depth, _, radii, grid_size = fields.shape
    first, count = halves
    rows = phase.shape[1] // 2
    piece = (rows // 8, 2, radii, 2 * depth)
    whole = lambda shape: pl.BlockSpec(shape, lambda i: (0,) * len(shape))
    return pl.pallas_call(
        functools.partial(azimuth_kernel, len(after)),
        grid=(count,),
        in_specs=[
            pl.BlockSpec((2, rows, grid_size), lambda i: (0, first + i, 0)),
            whole(swap.shape),
            pl.BlockSpec((depth, None, radii, grid_size), lambda i: (0, field, 0, 0)),
            *([pl.BlockSpec(memory_space=pl.ANY)] * len(after)),
        ],
        out_specs=[pl.BlockSpec(piece, lambda i: (0, i, 0, 0))] * 4,
        out_shape=[jax.ShapeDtypeStruct((piece[0], 2 * count, *piece[2:]), BF16)] * 4,
        scratch_shapes=[
            pltpu.VMEM((radii, 512 - depth, grid_size), BF16),
            pltpu.VMEM((rows, radii, 2 * depth), F32),
        ],
        compiler_params=params(48),
        cost_estimate=cost(micros),
        name="azimuth",
    )(phase, swap, fields, *after)


def join_kernel(*refs):
    for at, piece in enumerate(refs[:4]):
        refs[-1][:, at] = piece[...]


def join(pieces, *after, micros=0):
    steps = 2
    shape = pieces[0].shape
    block = (shape[0] // steps, *shape[1:])
    return pl.pallas_call(
        join_kernel,
        grid=(steps,),
        in_specs=[pl.BlockSpec(block, lambda i: (i, 0, 0, 0))] * 4
        + [pl.BlockSpec(memory_space=pl.ANY)] * len(after),
        out_specs=pl.BlockSpec((block[0], 4, *block[1:]), lambda i: (i, 0, 0, 0, 0)),
        out_shape=jax.ShapeDtypeStruct((shape[0], 4, *shape[1:]), BF16),
        compiler_params=params(62),
        cost_estimate=cost(micros),
        name="join",
    )(*pieces, *after)


def tie(x, *after, micros=0):
    anywhere = pl.BlockSpec(memory_space=pl.ANY)
    return pl.pallas_call(
        lambda *_: None,
        in_specs=[anywhere] * (1 + len(after)),
        out_specs=anywhere,
        out_shape=jax.ShapeDtypeStruct(x.shape, x.dtype),
        input_output_aliases={0: 0},
        cost_estimate=cost(micros),
        name="tie",
    )(x, *after)


def tables_kernel(own_ref, modes_ref, counts_ref, table_ref, *rest):
    out_ref = rest[-1]
    rows, size = out_ref.shape[1:]
    kept = counts_ref[modes_ref[pl.program_id(0)]]
    n_index = lax.broadcasted_iota(jnp.int32, (rows, 1), 0)
    for side in range(2):
        upper = own_ref[1] if side == 0 else 1 - own_ref[1]
        part = table_ref[:, upper].astype(F32).reshape(size, rows)
        out_ref[side] = jnp.where(n_index < kept, part.T, 0.0).astype(BF16)


def tables(own, modes, counts, radial_tables, radii, *after, micros=0):
    slots, radial_total, radial_size = radial_tables.shape
    slots //= 2
    split = (16, 2, 2, radii, radial_size)
    return pl.pallas_call(
        tables_kernel,
        grid_spec=pltpu.PrefetchScalarGridSpec(
            num_scalar_prefetch=3,
            grid=(slots,),
            in_specs=[
                pl.BlockSpec((None, *split), lambda i, own, *_: (own[0] * slots + i, 0, 0, 0, 0, 0)),
                *([pl.BlockSpec(memory_space=pl.ANY)] * len(after)),
            ],
            out_specs=pl.BlockSpec(
                (None, 2, radial_size, radial_total // 2), lambda i, *_: (i, 0, 0, 0)
            ),
        ),
        out_shape=jax.ShapeDtypeStruct((slots, 2, radial_size, radial_total // 2), BF16),
        compiler_params=params(62),
        cost_estimate=cost(micros),
        name="tables",
    )(own, modes, counts, radial_tables.reshape(2 * slots, *split), *after)


def vertical_kernel(own_ref, depth_ref, synth_ref, *rest):
    by_height, turned, depth_out, synth_out = rest[-1], rest[-2], rest[-4], rest[-3]
    local = synth_ref.shape[0] // 2
    pad = 256 - local
    by_height[...] = depth_ref[...].astype(F32).T.astype(BF16)
    turned[...] = synth_ref[...]
    zeros = jnp.zeros((pad, synth_ref.shape[0]), BF16)
    for side in range(2):
        group = own_ref[0] if side == 0 else 1 - own_ref[0]
        start = pl.multiple_of(group * local, local)
        part = by_height[pl.ds(start, local), :]
        depth_out[0, side, :local] = part
        depth_out[0, side, local:] = zeros
        depth_out[1, side, :pad] = zeros
        depth_out[1, side, pad:] = part
        synth_out[side * local : (side + 1) * local] = turned[pl.ds(start, local), :]


def vertical(own, depth_analysis, synthesis, *after, micros=0):
    fields, total, _ = depth_analysis.shape
    square = pl.BlockSpec((None, total, total), lambda i, *_: (i, 0, 0))
    return pl.pallas_call(
        vertical_kernel,
        grid_spec=pltpu.PrefetchScalarGridSpec(
            num_scalar_prefetch=1,
            grid=(fields,),
            in_specs=[square, square, *([pl.BlockSpec(memory_space=pl.ANY)] * len(after))],
            out_specs=[
                pl.BlockSpec((None, 2, 2, 256, total), lambda i, *_: (i, 0, 0, 0, 0)),
                square,
            ],
            scratch_shapes=[pltpu.VMEM((total, total), BF16)] * 2,
        ),
        out_shape=[
            jax.ShapeDtypeStruct((fields, 2, 2, 256, total), BF16),
            jax.ShapeDtypeStruct((fields, total, total), BF16),
        ],
        compiler_params=params(62),
        cost_estimate=cost(micros),
        name="vertical",
    )(own, depth_analysis, synthesis, *after)


def solve_kernel(first, part, place_ref, modes_ref, *rest):
    x, table_ref, depth_ref, synth_ref, tau_ref, step_ref = rest[:6]
    own_ref, other_ref, spread = rest[-3:]
    sources, _, some, radii, lanes = x.shape
    modes_here = table_ref.shape[2]
    half = synth_ref.shape[0] // 2
    quarter = half // 2
    near = 1 - place_ref[0]
    step = step_ref[0, 0]
    block = first + pl.program_id(0)
    n_index = lax.broadcasted_iota(jnp.int32, (modes_here, 1), 0) + block * modes_here
    tau = 1.0 + step * tau_ref[...]
    for q in range(some):
        projected = [None, None]
        for g, parts in enumerate((((0, 3), (1, 2)), ((near, 0), (1 - near, 1)))):
            radial = sum(
                dot(table_ref[q, side], x[:, at, q].reshape(sources * radii, lanes), NN)
                for side, at in parts
            ).astype(BF16)
            for p in range(2):
                term = dot(radial[:, p * 128 : p * 128 + 256], depth_ref[p, g], NN)
                projected[p] = term if g == 0 else projected[p] + term
        summed = modes_ref[q + (some if part == 1 else 0)] + 2 * n_index
        weight = (summed * (summed + 2)).astype(F32) * (step / float(512 * 512))
        scale = 1.0 / (weight + tau)
        for p in range(2):
            eigen = (projected[p] * scale).astype(BF16)
            found = dot(synth_ref[...], eigen, NT)
            at = 2 * q + p
            if part is None:
                spread[:, at, :] = found
                continue
            if part == 0:
                spread[:quarter, at, :] = found[:quarter]
                spread[:quarter, 4 + at, :] = found[quarter:half]
            else:
                spread[:half, 4 + at, :] = found[:half]
            spread[half : half + quarter, at, :] = found[half : half + quarter]
            spread[half : half + quarter, 4 + at, :] = found[half + quarter :]
    if part is None:
        own_ref[...] = spread[:half].astype(BF16)
        other_ref[...] = spread[half:].astype(BF16)
        return
    if part == 0:
        own_ref[...] = spread[:quarter].astype(BF16)
    else:
        early = rest[6][...].astype(F32)
        low, high = side_by_side(early, spread[:quarter], spread[quarter:half])
        own_ref[:quarter] = low.astype(BF16)
        own_ref[quarter:] = high.astype(BF16)
    other_ref[...] = spread[half : half + quarter].astype(BF16)


def side_by_side(early, low, high):
    row = lax.broadcasted_iota(jnp.int32, early.shape, 1)
    return jnp.where(row < 4, early, low), jnp.where(row < 4, pltpu.roll(early, 4, axis=1), high)


def solve(place, modes, x, table, depth, synth, tau, steps, field, out, blocks, *after, part=None, early=None, micros=0):
    depth_total = synth.shape[1]
    some, radial_size = x.shape[2], table.shape[2]
    half, cols = depth_total // 2, 8
    fields = synth.shape[0]
    block = 256
    first, count = blocks
    const = lambda shape: pl.BlockSpec(shape, lambda i, *_: (0,) * len(shape))
    of_field = lambda *shape: pl.BlockSpec((None, *shape), lambda i, *_: (field,) + (0,) * len(shape))
    slots_at = 1 if part == 1 else 0
    in_specs = [
        const(x.shape),
        pl.BlockSpec((some, 2, block, table.shape[3]), lambda i, *_: (slots_at, 0, first + i, 0)),
        of_field(*depth.shape[1:]),
        of_field(depth_total, depth_total),
        of_field(1, depth_total),
        of_field(1, 1),
    ]
    args = [place, modes, x, table, depth, synth, tau[:, None, :], steps[:, None, None]]
    packed = (half // 2, cols, block)
    if part == 1:
        in_specs.append(pl.BlockSpec(packed, lambda i, *_: (0, 0, first + i)))
        args.append(early)
    aliases = {}
    if out is not None:
        in_specs.append(pl.BlockSpec(memory_space=pl.ANY))
        args.append(out)
        aliases = {len(args) - 1: 0}
    in_specs += [pl.BlockSpec(memory_space=pl.ANY)] * len(after)
    args += after
    height = half if part is None else half // 2
    if part == 0:
        own_spec = pl.BlockSpec(packed, lambda i, *_: (0, 0, i))
        own_shape = (half // 2, cols, count * block)
    else:
        own_spec = pl.BlockSpec(
            (half, None, cols, block), lambda i, place, _: (0, field, place[0], first + i)
        )
        own_shape = (half, fields, 2 * cols, radial_size)
    return pl.pallas_call(
        functools.partial(solve_kernel, first, part),
        grid_spec=pltpu.PrefetchScalarGridSpec(
            num_scalar_prefetch=2,
            grid=(count,),
            in_specs=in_specs,
            out_specs=[own_spec, pl.BlockSpec((height, cols, block), lambda i, *_: (0, 0, i))],
            scratch_shapes=[pltpu.VMEM((depth_total, cols, block), F32)],
        ),
        out_shape=[
            jax.ShapeDtypeStruct(own_shape, BF16),
            jax.ShapeDtypeStruct((height, cols, count * block), BF16),
        ],
        input_output_aliases=aliases,
        compiler_params=params(62),
        cost_estimate=cost(micros),
        name="solve",
    )(*args)


def merge_kernel(place_ref, early_ref, late_ref, _, out_ref):
    quarter = early_ref.shape[0]
    late = late_ref[...].astype(F32)
    low, high = side_by_side(early_ref[...].astype(F32), pltpu.roll(late, 4, axis=1), late)
    out_ref[:quarter] = low.astype(BF16)
    out_ref[quarter:] = high.astype(BF16)


def merge(place, early, late, field, first, out, micros):
    packed = late.shape
    quarter, cols, block = packed
    return pl.pallas_call(
        merge_kernel,
        grid_spec=pltpu.PrefetchScalarGridSpec(
            num_scalar_prefetch=1,
            grid=(1,),
            in_specs=[
                pl.BlockSpec(packed, lambda i, _: (0, 0, first)),
                pl.BlockSpec(packed, lambda i, _: (0, 0, 0)),
                pl.BlockSpec(memory_space=pl.ANY),
            ],
            out_specs=pl.BlockSpec(
                (2 * quarter, None, cols, block), lambda i, place: (0, field, 1 - place[0], first)
            ),
        ),
        out_shape=jax.ShapeDtypeStruct(out.shape, BF16),
        input_output_aliases={3: 0},
        compiler_params=params(24),
        cost_estimate=cost(micros),
        name="merge",
    )(place, early, late, out)


def place_kernel(place_ref, received_ref, _, out_ref):
    out_ref[...] = received_ref[...]


def put(place, received, field, first, out, micros):
    half, cols, radial_size = received.shape
    return pl.pallas_call(
        place_kernel,
        grid_spec=pltpu.PrefetchScalarGridSpec(
            num_scalar_prefetch=1,
            grid=(1,),
            in_specs=[
                pl.BlockSpec((half, cols, radial_size), lambda i, _: (i, 0, 0)),
                pl.BlockSpec(memory_space=pl.ANY),
            ],
            out_specs=pl.BlockSpec(
                (half, None, cols, radial_size), lambda i, place: (i, field, 1 - place[0], first)
            ),
        ),
        out_shape=jax.ShapeDtypeStruct(out.shape, BF16),
        input_output_aliases={2: 0},
        compiler_params=params(24),
        cost_estimate=cost(micros),
        name="put",
    )(place, received, out)


def shards(
    fields,
    radial_tables,
    radial_counts,
    assignment,
    depth_analysis,
    synthesis,
    tau_values,
    time_steps,
):
    depth_local, field_count, radii, grid_size = fields.shape
    depth_total = depth_analysis.shape[1]
    mode_count = grid_size // 2
    block_count = assignment.shape[0]
    block_size = mode_count // block_count
    group, upper = lax.axis_index("xl"), lax.axis_index("xh")
    ring = lax.axis_index(("z", "y", "xh", "core"))
    place = group[None].astype(jnp.int32)
    inner = jnp.arange(block_size, dtype=jnp.int32)

    by_x = assignment.reshape(16, 2, 2, 2).transpose(1, 3, 0, 2).reshape(4, 32)
    by_x = lax.dynamic_slice_in_dim(jnp.concatenate([by_x, by_x]), 2 * upper + group, 4)
    ordered = jnp.stack([by_x[shift] for shift in SHIFTS])
    modes_to = ordered[None, :, :, None] * block_size + inner.reshape(2, 1, 1, 2)
    modes_to = modes_to.reshape(mode_count)
    phase = phase_rows(modes_to, grid_size)
    index = jnp.arange(256, dtype=jnp.int32)
    heights = 256 // radii
    origin = (index % heights) * radii + index // heights
    swap = (origin[:, None] == index[None, :]).astype(BF16)

    def along_x(pieces):
        return [along(x, shift) for x, shift in zip(pieces, SHIFTS[:3], strict=True)]

    def across(x):
        return lax.all_to_all(x, ("z", "y", "core"), 0, 0, tiled=True)

    def solved(x, field, out, blocks, *after, **options):
        operands = (table, depth, synth, tau_values, time_steps, field, out, blocks)
        out, other = solve(place, modes_here, x, *operands, *after, **options)
        return out, lax.ppermute(other, "xl", [(0, 1), (1, 0)])

    def sent_of(field, halves, *after, **options):
        *moving, own = azimuth(phase, swap, fields, field, halves, *after, **options)
        return [*along_x(moving), own]

    whole, low_n, high_n = (0, 2), (0, 1), (1, 1)
    a = sent_of(0, (0, 1))
    b = sent_of(1, whole, a[3], micros=COSTS["azB"])
    a = join(a, b[3], micros=COSTS["joinA"])
    c = sent_of(2, whole, a, micros=COSTS["azC"])
    a = across(a)
    b = join(b, c[3], micros=COSTS["joinB"])

    own = jnp.stack([group, upper]).astype(jnp.int32)
    own_block = lax.dynamic_slice_in_dim(assignment, ring * 2 + group, 1)
    modes_here = own_block * block_size + inner
    depth, synth = vertical(own, depth_analysis, synthesis, b, micros=COSTS["vertical"])
    d = sent_of(0, (1, 1), depth, micros=COSTS["azD"])
    table = tables(own, modes_here, radial_counts, radial_tables, radii, d[3], micros=COSTS["tables"])

    b = across(b)
    c = join(c, table, depth, synth, micros=COSTS["joinC"])
    early, other_a = solved(a, 0, None, whole, c, part=0, micros=COSTS["sA"])
    c = across(c)
    out, other1a = solved(b, 1, None, low_n, early, micros=COSTS["s1a"])
    out, other1b = solved(b, 1, out, high_n, micros=COSTS["s1b"])
    d = join(d, out, micros=COSTS["joinD"])
    out, other2a = solved(c, 2, out, low_n, other_a, micros=COSTS["s2a"])
    d = across(tie(d, out, micros=COSTS["tie"]))
    out, other2b = solved(c, 2, out, high_n, micros=COSTS["s2b"])
    out = put(place, other1a, 1, 0, out, micros=COSTS["p1a"])
    out = put(place, other1b, 1, 1, out, micros=COSTS["p1b"])
    out = put(place, other2a, 2, 0, out, micros=COSTS["p2a"])
    out, other_da = solved(d, 0, out, low_n, part=1, early=early, micros=COSTS["sDa"])
    out, other_db = solved(d, 0, out, high_n, part=1, early=early, micros=COSTS["sDb"])
    out = put(place, other2b, 2, 1, out, micros=COSTS["p2b"])
    out = merge(place, other_a, other_da, 0, 0, out, micros=COSTS["mDa"])
    return merge(place, other_a, other_db, 0, 1, out, micros=COSTS["mDb"])


def solution(mesh):
    split = Mesh(mesh.devices.reshape(2, 4, 4, 2, 2), ("xl", "z", "y", "xh", "core"))
    ma = ("z", "y", "xh", "core")
    placed = (P("xl", None, ma, None), P(ma, None, None), P(), P(), P(), P(), P(), P())
    return jax.shard_map(
        shards, mesh=split, in_specs=placed, out_specs=P("xl", None, ma, None), check_vma=False
    )
```

```python
import functools
import math

import jax
import jax.numpy as jnp
from jax import lax
from jax.experimental import pallas as pl
from jax.experimental.pallas import tpu as pltpu
from jax.sharding import Mesh
from jax.sharding import PartitionSpec as P

F32, BF16 = jnp.float32, jnp.bfloat16
NT = (((1,), (1,)), ((), ()))
NN = (((1,), (0,)), ((), ()))
MIB = 1 << 20


def cost(micros):
    return pl.CostEstimate(flops=micros * 10**9, bytes_accessed=1000, transcendentals=0)


COSTS = {'tie': 0, 'vertical': 80, 'tables': 0, 'azB': 0, 'azC': 20, 'azD': 0, 'joinA': 0, 'joinB': 20, 'joinC': 0, 'joinD': 2, 'sA': 0, 's1a': 0, 's1b': 40, 's2a': 0, 's2m': 0, 'p2m': 0, 's2b': 0, 'sDa': 0, 'sDb': 0, 'p1a': 1, 'p1b': 1, 'p2a': 30, 'p2b': 1, 'mDa': 1, 'mDb': 1}
SHORT = cost(0)
SHIFTS = (1, 3, 2, 0)


def along(x, shift):
    at = lambda chip: (chip % 2) * 2 + chip // 2
    return lax.ppermute(x, ("xl", "xh"), [(at(i), at((i + shift) % 4)) for i in range(4)])


def dot(a, b, dims):
    return lax.dot_general(a, b, dims, preferred_element_type=F32)


def params(mib):
    return pltpu.CompilerParams(vmem_limit_bytes=mib * MIB)


def phase_kernel(c0_ref, s0_ref, c1_ref, s1_ref, out_ref):
    c0, s0 = c0_ref[...], s0_ref[...]
    width = c0.shape[1]
    for block in range(out_ref.shape[2] // width):
        c1, s1 = c1_ref[:, block : block + 1], s1_ref[:, block : block + 1]
        lanes = slice(block * width, (block + 1) * width)
        out_ref[0, :, lanes] = (c0 * c1 - s0 * s1).astype(BF16)
        out_ref[1, :, lanes] = -(s0 * c1 + c0 * s1).astype(BF16)


def phase_rows(modes, grid_size):
    width = 128

    def tables(points, scale):
        index = (modes[:, None] * points[None, :]) % grid_size
        angle = index.astype(F32) * (2.0 * math.pi / grid_size)
        return jnp.cos(angle) * scale, jnp.sin(angle) * scale

    c0, s0 = tables(jnp.arange(width, dtype=jnp.int32), math.sqrt(2.0 / grid_size))
    c1, s1 = tables(jnp.arange(grid_size // width, dtype=jnp.int32) * width, 1.0)
    return pl.pallas_call(
        phase_kernel,
        out_shape=jax.ShapeDtypeStruct((2, modes.shape[0], grid_size), BF16),
        compiler_params=params(40),
        cost_estimate=SHORT,
        name="phase_table",
    )(c0, s0, c1, s1)


def azimuth_kernel(many, phase_ref, swap_ref, x_ref, *rest):
    outs, (rows, spread) = rest[many:-2], rest[-2:]
    depth, radii, grid_size = x_ref.shape
    pad = 256 - depth
    group = 256 // radii

    @pl.when(pl.program_id(0) == 0)
    def _():
        zeros = jnp.zeros((pad, grid_size), BF16)
        for r in range(radii):
            rows[r, 0:pad] = zeros
            rows[r, pad + depth :] = zeros
        for block in range(depth // group):
            heights = slice(block * group, (block + 1) * group)
            swapped = dot(swap_ref[...], x_ref[heights].reshape(256, grid_size), NN).astype(BF16)
            for r in range(radii):
                start = pad + block * group
                rows[r, start : start + group] = swapped[r * group : (r + 1) * group]

    for r in range(radii):
        cosine = dot(phase_ref[0], rows[r, pad:], NT)
        sine = dot(phase_ref[1], rows[r, 0:256], NT)
        spread[:, r, 0:128] = cosine[:, :128]
        spread[:, r, 128:256] = cosine[:, 128:] + sine[:, :128]
        spread[:, r, 256:384] = sine[:, 128:]
    count = spread.shape[0] // len(outs)
    for j, out in enumerate(outs):
        piece = spread[j * count : (j + 1) * count].astype(BF16)
        out[...] = piece.reshape(out.shape)


def azimuth(phase, swap, fields, field, halves, *after, micros=0):
    depth, _, radii, grid_size = fields.shape
    first, count = halves
    rows = phase.shape[1] // 2
    piece = (rows // 8, 2, radii, 2 * depth)
    whole = lambda shape: pl.BlockSpec(shape, lambda i: (0,) * len(shape))
    return pl.pallas_call(
        functools.partial(azimuth_kernel, len(after)),
        grid=(count,),
        in_specs=[
            pl.BlockSpec((2, rows, grid_size), lambda i: (0, first + i, 0)),
            whole(swap.shape),
            pl.BlockSpec((depth, None, radii, grid_size), lambda i: (0, field, 0, 0)),
            *([pl.BlockSpec(memory_space=pl.ANY)] * len(after)),
        ],
        out_specs=[pl.BlockSpec(piece, lambda i: (0, i, 0, 0))] * 4,
        out_shape=[jax.ShapeDtypeStruct((piece[0], 2 * count, *piece[2:]), BF16)] * 4,
        scratch_shapes=[
            pltpu.VMEM((radii, 512 - depth, grid_size), BF16),
            pltpu.VMEM((rows, radii, 2 * depth), F32),
        ],
        compiler_params=params(48),
        cost_estimate=cost(micros),
        name="azimuth",
    )(phase, swap, fields, *after)


def join_kernel(*refs):
    for at, piece in enumerate(refs[:4]):
        refs[-1][:, at] = piece[...]


def join(pieces, *after, micros=0):
    steps = 2
    shape = pieces[0].shape
    block = (shape[0] // steps, *shape[1:])
    return pl.pallas_call(
        join_kernel,
        grid=(steps,),
        in_specs=[pl.BlockSpec(block, lambda i: (i, 0, 0, 0))] * 4
        + [pl.BlockSpec(memory_space=pl.ANY)] * len(after),
        out_specs=pl.BlockSpec((block[0], 4, *block[1:]), lambda i: (i, 0, 0, 0, 0)),
        out_shape=jax.ShapeDtypeStruct((shape[0], 4, *shape[1:]), BF16),
        compiler_params=params(62),
        cost_estimate=cost(micros),
        name="join",
    )(*pieces, *after)


def tie(x, *after, micros=0):
    anywhere = pl.BlockSpec(memory_space=pl.ANY)
    return pl.pallas_call(
        lambda *_: None,
        in_specs=[anywhere] * (1 + len(after)),
        out_specs=anywhere,
        out_shape=jax.ShapeDtypeStruct(x.shape, x.dtype),
        input_output_aliases={0: 0},
        cost_estimate=cost(micros),
        name="tie",
    )(x, *after)


def tables_kernel(own_ref, modes_ref, counts_ref, table_ref, *rest):
    out_ref = rest[-1]
    rows, size = out_ref.shape[1:]
    kept = counts_ref[modes_ref[pl.program_id(0)]]
    n_index = lax.broadcasted_iota(jnp.int32, (rows, 1), 0)
    for side in range(2):
        upper = own_ref[1] if side == 0 else 1 - own_ref[1]
        part = table_ref[:, upper].astype(F32).reshape(size, rows)
        out_ref[side] = jnp.where(n_index < kept, part.T, 0.0).astype(BF16)


def tables(own, modes, counts, radial_tables, radii, *after, micros=0):
    slots, radial_total, radial_size = radial_tables.shape
    slots //= 2
    split = (16, 2, 2, radii, radial_size)
    return pl.pallas_call(
        tables_kernel,
        grid_spec=pltpu.PrefetchScalarGridSpec(
            num_scalar_prefetch=3,
            grid=(slots,),
            in_specs=[
                pl.BlockSpec((None, *split), lambda i, own, *_: (own[0] * slots + i, 0, 0, 0, 0, 0)),
                *([pl.BlockSpec(memory_space=pl.ANY)] * len(after)),
            ],
            out_specs=pl.BlockSpec(
                (None, 2, radial_size, radial_total // 2), lambda i, *_: (i, 0, 0, 0)
            ),
        ),
        out_shape=jax.ShapeDtypeStruct((slots, 2, radial_size, radial_total // 2), BF16),
        compiler_params=params(62),
        cost_estimate=cost(micros),
        name="tables",
    )(own, modes, counts, radial_tables.reshape(2 * slots, *split), *after)


def vertical_kernel(own_ref, depth_ref, synth_ref, *rest):
    by_height, turned, depth_out, synth_out = rest[-1], rest[-2], rest[-4], rest[-3]
    local = synth_ref.shape[0] // 2
    pad = 256 - local
    by_height[...] = depth_ref[...].astype(F32).T.astype(BF16)
    turned[...] = synth_ref[...]
    zeros = jnp.zeros((pad, synth_ref.shape[0]), BF16)
    for side in range(2):
        group = own_ref[0] if side == 0 else 1 - own_ref[0]
        start = pl.multiple_of(group * local, local)
        part = by_height[pl.ds(start, local), :]
        depth_out[0, side, :local] = part
        depth_out[0, side, local:] = zeros
        depth_out[1, side, :pad] = zeros
        depth_out[1, side, pad:] = part
        synth_out[side * local : (side + 1) * local] = turned[pl.ds(start, local), :]


def vertical(own, depth_analysis, synthesis, *after, micros=0):
    fields, total, _ = depth_analysis.shape
    square = pl.BlockSpec((None, total, total), lambda i, *_: (i, 0, 0))
    return pl.pallas_call(
        vertical_kernel,
        grid_spec=pltpu.PrefetchScalarGridSpec(
            num_scalar_prefetch=1,
            grid=(fields,),
            in_specs=[square, square, *([pl.BlockSpec(memory_space=pl.ANY)] * len(after))],
            out_specs=[
                pl.BlockSpec((None, 2, 2, 256, total), lambda i, *_: (i, 0, 0, 0, 0)),
                square,
            ],
            scratch_shapes=[pltpu.VMEM((total, total), BF16)] * 2,
        ),
        out_shape=[
            jax.ShapeDtypeStruct((fields, 2, 2, 256, total), BF16),
            jax.ShapeDtypeStruct((fields, total, total), BF16),
        ],
        compiler_params=params(62),
        cost_estimate=cost(micros),
        name="vertical",
    )(own, depth_analysis, synthesis, *after)


def solve_kernel(first, part, place_ref, modes_ref, *rest):
    x, table_ref, depth_ref, synth_ref, tau_ref, step_ref = rest[:6]
    own_ref, other_ref, spread = rest[-3:]
    sources, _, some, radii, lanes = x.shape
    modes_here = table_ref.shape[2]
    half = synth_ref.shape[0] // 2
    quarter = half // 2
    near = 1 - place_ref[0]
    step = step_ref[0, 0]
    block = first + pl.program_id(0)
    n_index = lax.broadcasted_iota(jnp.int32, (modes_here, 1), 0) + block * modes_here
    tau = 1.0 + step * tau_ref[...]
    for q in range(some):
        projected = [None, None]
        for g, parts in enumerate((((0, 3), (1, 2)), ((near, 0), (1 - near, 1)))):
            radial = sum(
                dot(table_ref[q, side], x[:, at, q].reshape(sources * radii, lanes), NN)
                for side, at in parts
            ).astype(BF16)
            for p in range(2):
                term = dot(radial[:, p * 128 : p * 128 + 256], depth_ref[p, g], NN)
                projected[p] = term if g == 0 else projected[p] + term
        summed = modes_ref[q + (some if part == 1 else 0)] + 2 * n_index
        weight = (summed * (summed + 2)).astype(F32) * (step / float(512 * 512))
        scale = 1.0 / (weight + tau)
        for p in range(2):
            eigen = (projected[p] * scale).astype(BF16)
            found = dot(synth_ref[...], eigen, NT)
            at = 2 * q + p
            if part is None:
                spread[:, at, :] = found
                continue
            if part == 0:
                spread[:quarter, at, :] = found[:quarter]
                spread[:quarter, 4 + at, :] = found[quarter:half]
            else:
                spread[:half, 4 + at, :] = found[:half]
            spread[half : half + quarter, at, :] = found[half : half + quarter]
            spread[half : half + quarter, 4 + at, :] = found[half + quarter :]
    if part is None:
        own_ref[...] = spread[:half].astype(BF16)
        other_ref[...] = spread[half:].astype(BF16)
        return
    if part == 0:
        own_ref[...] = spread[:quarter].astype(BF16)
    else:
        early = rest[6][...].astype(F32)
        low, high = side_by_side(early, spread[:quarter], spread[quarter:half])
        own_ref[:quarter] = low.astype(BF16)
        own_ref[quarter:] = high.astype(BF16)
    other_ref[...] = spread[half : half + quarter].astype(BF16)


def side_by_side(early, low, high):
    row = lax.broadcasted_iota(jnp.int32, early.shape, 1)
    return jnp.where(row < 4, early, low), jnp.where(row < 4, pltpu.roll(early, 4, axis=1), high)


def solve(place, modes, x, table, depth, synth, tau, steps, field, out, blocks, *after, part=None, early=None, micros=0):
    depth_total = synth.shape[1]
    some, radial_size = x.shape[2], table.shape[2]
    half, cols = depth_total // 2, 8
    fields = synth.shape[0]
    first, count, block = blocks
    const = lambda shape: pl.BlockSpec(shape, lambda i, *_: (0,) * len(shape))
    of_field = lambda *shape: pl.BlockSpec((None, *shape), lambda i, *_: (field,) + (0,) * len(shape))
    slots_at = 1 if part == 1 else 0
    in_specs = [
        const(x.shape),
        pl.BlockSpec((some, 2, block, table.shape[3]), lambda i, *_: (slots_at, 0, first + i, 0)),
        of_field(*depth.shape[1:]),
        of_field(depth_total, depth_total),
        of_field(1, depth_total),
        of_field(1, 1),
    ]
    args = [place, modes, x, table, depth, synth, tau[:, None, :], steps[:, None, None]]
    packed = (half // 2, cols, block)
    if part == 1:
        in_specs.append(pl.BlockSpec(packed, lambda i, *_: (0, 0, first + i)))
        args.append(early)
    aliases = {}
    if out is not None:
        in_specs.append(pl.BlockSpec(memory_space=pl.ANY))
        args.append(out)
        aliases = {len(args) - 1: 0}
    in_specs += [pl.BlockSpec(memory_space=pl.ANY)] * len(after)
    args += after
    height = half if part is None else half // 2
    if part == 0:
        own_spec = pl.BlockSpec(packed, lambda i, *_: (0, 0, i))
        own_shape = (half // 2, cols, count * block)
    else:
        own_spec = pl.BlockSpec(
            (half, None, cols, block), lambda i, place, _: (0, field, place[0], first + i)
        )
        own_shape = (half, fields, 2 * cols, radial_size)
    return pl.pallas_call(
        functools.partial(solve_kernel, first, part),
        grid_spec=pltpu.PrefetchScalarGridSpec(
            num_scalar_prefetch=2,
            grid=(count,),
            in_specs=in_specs,
            out_specs=[own_spec, pl.BlockSpec((height, cols, block), lambda i, *_: (0, 0, i))],
            scratch_shapes=[pltpu.VMEM((depth_total, cols, block), F32)],
        ),
        out_shape=[
            jax.ShapeDtypeStruct(own_shape, BF16),
            jax.ShapeDtypeStruct((height, cols, count * block), BF16),
        ],
        input_output_aliases=aliases,
        compiler_params=params(62),
        cost_estimate=cost(micros),
        name="solve",
    )(*args)


def merge_kernel(place_ref, early_ref, late_ref, _, out_ref):
    quarter = early_ref.shape[0]
    late = late_ref[...].astype(F32)
    low, high = side_by_side(early_ref[...].astype(F32), pltpu.roll(late, 4, axis=1), late)
    out_ref[:quarter] = low.astype(BF16)
    out_ref[quarter:] = high.astype(BF16)


def merge(place, early, late, field, first, out, micros):
    packed = late.shape
    quarter, cols, block = packed
    return pl.pallas_call(
        merge_kernel,
        grid_spec=pltpu.PrefetchScalarGridSpec(
            num_scalar_prefetch=1,
            grid=(1,),
            in_specs=[
                pl.BlockSpec(packed, lambda i, _: (0, 0, first)),
                pl.BlockSpec(packed, lambda i, _: (0, 0, 0)),
                pl.BlockSpec(memory_space=pl.ANY),
            ],
            out_specs=pl.BlockSpec(
                (2 * quarter, None, cols, block), lambda i, place: (0, field, 1 - place[0], first)
            ),
        ),
        out_shape=jax.ShapeDtypeStruct(out.shape, BF16),
        input_output_aliases={3: 0},
        compiler_params=params(24),
        cost_estimate=cost(micros),
        name="merge",
    )(place, early, late, out)


def place_kernel(place_ref, received_ref, _, out_ref):
    out_ref[...] = received_ref[...]


def put(place, received, field, first, out, micros):
    half, cols, radial_size = received.shape
    return pl.pallas_call(
        place_kernel,
        grid_spec=pltpu.PrefetchScalarGridSpec(
            num_scalar_prefetch=1,
            grid=(1,),
            in_specs=[
                pl.BlockSpec((half, cols, radial_size), lambda i, _: (i, 0, 0)),
                pl.BlockSpec(memory_space=pl.ANY),
            ],
            out_specs=pl.BlockSpec(
                (half, None, cols, radial_size), lambda i, place: (i, field, 1 - place[0], first)
            ),
        ),
        out_shape=jax.ShapeDtypeStruct(out.shape, BF16),
        input_output_aliases={2: 0},
        compiler_params=params(24),
        cost_estimate=cost(micros),
        name="put",
    )(place, received, out)


def shards(
    fields,
    radial_tables,
    radial_counts,
    assignment,
    depth_analysis,
    synthesis,
    tau_values,
    time_steps,
):
    depth_local, field_count, radii, grid_size = fields.shape
    depth_total = depth_analysis.shape[1]
    mode_count = grid_size // 2
    block_count = assignment.shape[0]
    block_size = mode_count // block_count
    group, upper = lax.axis_index("xl"), lax.axis_index("xh")
    ring = lax.axis_index(("z", "y", "xh", "core"))
    place = group[None].astype(jnp.int32)
    inner = jnp.arange(block_size, dtype=jnp.int32)

    by_x = assignment.reshape(16, 2, 2, 2).transpose(1, 3, 0, 2).reshape(4, 32)
    by_x = lax.dynamic_slice_in_dim(jnp.concatenate([by_x, by_x]), 2 * upper + group, 4)
    ordered = jnp.stack([by_x[shift] for shift in SHIFTS])
    modes_to = ordered[None, :, :, None] * block_size + inner.reshape(2, 1, 1, 2)
    modes_to = modes_to.reshape(mode_count)
    phase = phase_rows(modes_to, grid_size)
    index = jnp.arange(256, dtype=jnp.int32)
    heights = 256 // radii
    origin = (index % heights) * radii + index // heights
    swap = (origin[:, None] == index[None, :]).astype(BF16)

    def along_x(pieces):
        return [along(x, shift) for x, shift in zip(pieces, SHIFTS[:3], strict=True)]

    def across(x):
        return lax.all_to_all(x, ("z", "y", "core"), 0, 0, tiled=True)

    def solved(x, field, out, blocks, *after, **options):
        operands = (table, depth, synth, tau_values, time_steps, field, out, blocks)
        out, other = solve(place, modes_here, x, *operands, *after, **options)
        return out, lax.ppermute(other, "xl", [(0, 1), (1, 0)])

    def sent_of(field, halves, *after, **options):
        *moving, own = azimuth(phase, swap, fields, field, halves, *after, **options)
        return [*along_x(moving), own]

    whole, all_n, low_n, high_n = (0, 2), (0, 2, 256), (0, 1, 256), (1, 1, 256)
    a = sent_of(0, (0, 1))
    b = sent_of(1, whole, a[3], micros=COSTS["azB"])
    a = join(a, b[3], micros=COSTS["joinA"])
    c = sent_of(2, whole, a, micros=COSTS["azC"])
    a = across(a)
    b = join(b, c[3], micros=COSTS["joinB"])

    own = jnp.stack([group, upper]).astype(jnp.int32)
    own_block = lax.dynamic_slice_in_dim(assignment, ring * 2 + group, 1)
    modes_here = own_block * block_size + inner
    depth, synth = vertical(own, depth_analysis, synthesis, b, micros=COSTS["vertical"])
    d = sent_of(0, (1, 1), depth, micros=COSTS["azD"])
    table = tables(own, modes_here, radial_counts, radial_tables, radii, d[3], micros=COSTS["tables"])

    b = across(b)
    c = join(c, table, depth, synth, micros=COSTS["joinC"])
    early, other_a = solved(a, 0, None, all_n, c, part=0, micros=COSTS["sA"])
    c = across(c)
    out, other1a = solved(b, 1, None, low_n, early, micros=COSTS["s1a"])
    out, other1b = solved(b, 1, out, high_n, micros=COSTS["s1b"])
    d = join(d, out, micros=COSTS["joinD"])
    out, other2a = solved(c, 2, out, (0, 1, 128), other_a, micros=COSTS["s2a"])
    d = across(tie(d, out, micros=COSTS["tie"]))
    out, other2m = solved(c, 2, out, (1, 1, 128), micros=COSTS["s2m"])
    out, other2b = solved(c, 2, out, high_n, micros=COSTS["s2b"])
    out = put(place, other1a, 1, 0, out, micros=COSTS["p1a"])
    out = put(place, other1b, 1, 1, out, micros=COSTS["p1b"])
    out = put(place, other2a, 2, 0, out, micros=COSTS["p2a"])
    out = put(place, other2m, 2, 1, out, micros=COSTS["p2m"])
    out, other_da = solved(d, 0, out, low_n, part=1, early=early, micros=COSTS["sDa"])
    out, other_db = solved(d, 0, out, high_n, part=1, early=early, micros=COSTS["sDb"])
    out = put(place, other2b, 2, 1, out, micros=COSTS["p2b"])
    out = merge(place, other_a, other_da, 0, 0, out, micros=COSTS["mDa"])
    return merge(place, other_a, other_db, 0, 1, out, micros=COSTS["mDb"])


def solution(mesh):
    split = Mesh(mesh.devices.reshape(2, 4, 4, 2, 2), ("xl", "z", "y", "xh", "core"))
    ma = ("z", "y", "xh", "core")
    placed = (P("xl", None, ma, None), P(ma, None, None), P(), P(), P(), P(), P(), P())
    return jax.shard_map(
        shards, mesh=split, in_specs=placed, out_specs=P("xl", None, ma, None), check_vma=False
    )
```
